32 devices in a mesh: groups: 2 (over x), row: 16 (over z, y, core).
Axes of the slice: x: 2, y: 2, z: 4, core: 2. Of those that a mesh axis runs over, the one named last changes fastest.
Arguments:
- alignment_features: bfloat16 [64, 128, 64], P(('groups', 'row')), parts along dimension 0
- pair_features: bfloat16 [256, 128, 128], P(('groups', 'row')), parts along dimension 0
- token_residue_kind: int32 [256], P('groups'), parts along dimension 0, may hold values from 0 to 31
- alignment_mask: int32 [64], P('groups'), parts along dimension 0, may hold values from 0 to 1, as said below
- residue_embedding_table: bfloat16 [32, 64], replicated, may hold values from -0.099609375 to 0.099609375
- outer_left_weight: bfloat16 [64, 32], replicated, may hold values from -0.75 to 0.75
- outer_right_weight: bfloat16 [64, 32], replicated, may hold values from -0.75 to 0.75
- outer_output_weight: bfloat16 [1024, 128], replicated
- averaging_value_weight: bfloat16 [64, 256], replicated, may hold values from -0.75 to 0.75
- averaging_gate_weight: bfloat16 [64, 256], replicated, may hold values from -0.75 to 0.75
- averaging_head_logits: bfloat16 [128, 8], replicated
- averaging_output_weight: bfloat16 [256, 64], replicated, may hold values from -0.375 to 0.375
- triangle_projection_weight: bfloat16 [128, 512], replicated, may hold values from -0.5 to 0.5
- triangle_gate_weight: bfloat16 [128, 128], replicated, may hold values from -0.5 to 0.5
- triangle_output_weight: bfloat16 [128, 128], replicated, may hold values from -1.5 to 1.5
Outputs:
- alignment_output: bfloat16 [64, 128, 64], P(('groups', 'row')), parts along dimension 0
- pair_output: bfloat16 [256, 128, 128], P(('groups', 'row')), parts along dimension 0
The draws below stay inside these ranges and needn't reach their ends.
There are 2 independent parts, one for each index of `groups`. The reference program is written for one: setup_inputs(seed, part) draws one part's arguments, and reference() takes and returns one part's arrays. A program takes and returns all parts, laid end to end along the dimension named above; an argument that names none is the same for every part. Nothing has to cross between parts.
Inputs may be any that keep to these rules, and one draw needn't show every extreme that they name: `alignment_mask`: the first sequence is always valid.
All inputs are finite; a program needn't handle non-finite values.
Results may differ from the reference program's by a relative error of at most 0.038.
Values may be sent and summed in bfloat16 or wider, within the bound.
A program may use at most 64 MiB of HBM per device.

```python
import math
import jax
import jax.numpy as jnp
from jax import lax

CM = 64
CZ = 128
COPM = 32
HEADS = 8
HDIM = 32
CT = 128
RESTYPES = 32
N = 128
S = 32


def log_scale(key, array_shape, low, high):
    return jnp.exp(jax.random.uniform(key, array_shape, jnp.float32, math.log(low), math.log(high)))


def scaled_field(key, base, row_low, row_high):
    array_shape = base.shape
    keys = jax.random.split(key, 2)
    row_scale = log_scale(keys[0], array_shape[:-1] + (1,), row_low, row_high)
    column_scale = log_scale(keys[1], (array_shape[-1],), 0.4, 4.0)
    return base * row_scale * column_scale


def draw_alignment_features(key, part):
    key = jax.random.fold_in(key, 3)
    keys = jax.random.split(key, 2)
    base = jnp.clip(jax.random.normal(keys[0], (S, N, CM), jnp.float32), -4.0, 4.0)
    return scaled_field(keys[1], base, 0.02, 0.1).astype(jnp.bfloat16)


def draw_pair_features(key, part):
    key = jax.random.fold_in(key, 11)
    keys = jax.random.split(key, 2)
    base = jnp.clip(jax.random.normal(keys[0], (N, N, CZ), jnp.float32), -4.0, 4.0)
    return scaled_field(keys[1], base, 0.3, 0.8).astype(jnp.bfloat16)


def draw_outer_output_weight(key, part):
    key = jax.random.fold_in(key, 41)
    matrix = 8.0 / COPM * jnp.clip(jax.random.normal(key, (COPM * COPM, CZ), jnp.float32), -6.0, 6.0)
    return matrix.astype(jnp.bfloat16)


def draw_averaging_head_logits(key, part):
    keys = jax.random.split(jax.random.fold_in(key, 21), 2)
    return (0.18 * jnp.clip(jax.random.normal(keys[1], (CZ, HEADS), jnp.float32), -4.0, 4.0)).astype(jnp.bfloat16)


def draw_alignment_mask(key, part):
    flags = (jax.random.randint(jax.random.fold_in(key, 31), (S,), 0, 4) >= 1).astype(jnp.int32)
    return flags.at[0].set(1)


def place_ends(array, rng, smallest, largest):
    extent = array.shape
    spot = [jax.random.randint(jax.random.fold_in(rng, axis), (), 0, extent[axis]) for axis in range(len(extent))]
    array = array.at[tuple(spot)].set(smallest)
    longest = extent.index(max(extent))
    spot[longest] = (spot[longest] + 1) % extent[longest]
    return array.at[tuple(spot)].set(largest)


def normal_values(rng, shape, scale, limit, kind=jnp.bfloat16):
    entries = jax.random.normal(rng, shape, jnp.float32) * scale
    return jnp.minimum(jnp.maximum(entries, -limit), limit).astype(kind)


def setup_inputs(seed: int = 0, part: int = 0) -> dict:
    key_of = jax.random.split(jax.random.key(seed), 16)
    own_keys = jax.random.split(jax.random.fold_in(key_of[15], part), 16)
    return {
        "alignment_features": draw_alignment_features(jax.random.fold_in(jax.random.fold_in(key_of[15], part), 71), part),
        "pair_features": draw_pair_features(jax.random.fold_in(jax.random.fold_in(key_of[15], part), 71), part),
        "token_residue_kind": place_ends(jax.random.randint(own_keys[2], (N,), 0, RESTYPES), jax.random.fold_in(own_keys[2], 1), 0, RESTYPES - 1).astype(jnp.int32),
        "alignment_mask": draw_alignment_mask(jax.random.fold_in(jax.random.fold_in(key_of[15], part), 71), part),
        "residue_embedding_table": jnp.clip(jax.random.uniform(key_of[4], (RESTYPES, CM), jnp.float32, -0.099609375, 0.099609375), -0.099609375, 0.099609375).astype(jnp.bfloat16),
        "outer_left_weight": normal_values(key_of[5], (CM, COPM), CM ** -0.5, 0.75),
        "outer_right_weight": normal_values(key_of[6], (CM, COPM), CM ** -0.5, 0.75),
        "outer_output_weight": draw_outer_output_weight(jax.random.fold_in(key_of[15], 71), part),
        "averaging_value_weight": normal_values(key_of[8], (CM, HEADS * HDIM), CM ** -0.5, 0.75),
        "averaging_gate_weight": normal_values(key_of[9], (CM, HEADS * HDIM), CM ** -0.5, 0.75),
        "averaging_head_logits": draw_averaging_head_logits(jax.random.fold_in(key_of[15], 71), part),
        "averaging_output_weight": normal_values(key_of[11], (HEADS * HDIM, CM), (HEADS * HDIM) ** -0.5, 0.375),
        "triangle_projection_weight": normal_values(key_of[12], (CZ, 4 * CT), CZ ** -0.5, 0.5),
        "triangle_gate_weight": normal_values(key_of[13], (CZ, CZ), CZ ** -0.5, 0.5),
        "triangle_output_weight": normal_values(key_of[14], (CT, CZ), (CT // 8) ** -0.5, 1.5),
    }


def layer_normalize(inputs, axis):
    average = lax.optimization_barrier(jnp.mean(inputs, axis=axis, keepdims=True))
    centered = inputs - average
    variance = lax.optimization_barrier(jnp.mean(centered * centered, axis=axis, keepdims=True))
    return centered * lax.rsqrt(variance + 1e-05)

def reference(alignment_features, pair_features, token_residue_kind, alignment_mask, residue_embedding_table, outer_left_weight, outer_right_weight, outer_output_weight, averaging_value_weight, averaging_gate_weight, averaging_head_logits, averaging_output_weight, triangle_projection_weight, triangle_gate_weight, triangle_output_weight):
    one_hot = (token_residue_kind[:, None] == jnp.arange(RESTYPES, dtype=jnp.int32)[None, :]).astype(jnp.bfloat16)
    embedded_input = jnp.dot(one_hot, residue_embedding_table, preferred_element_type=jnp.float32)
    alignment_start = (alignment_features.astype(jnp.float32) + embedded_input[None]).astype(jnp.bfloat16)
    alignment_normalized = layer_normalize(alignment_start.astype(jnp.float32), 2).astype(jnp.bfloat16)
    mask_as_float = alignment_mask.astype(jnp.float32)
    left_projected_rows = (jnp.dot(alignment_normalized, outer_left_weight, preferred_element_type=jnp.float32) * mask_as_float[:, None, None]).astype(jnp.bfloat16)
    right_projected_rows = jnp.dot(alignment_normalized, outer_right_weight, preferred_element_type=jnp.float32).astype(jnp.bfloat16)
    seq_count = jnp.sum(mask_as_float)
    right_flat = right_projected_rows.reshape(S, N * COPM)
    opm_weight = outer_output_weight.astype(jnp.float32).reshape(COPM, COPM, CZ)

    def outer_block(left_row):
        summed = jnp.dot(left_row.T, right_flat, preferred_element_type=jnp.float32)
        product = (summed / seq_count).astype(jnp.bfloat16).reshape(COPM, N, COPM)
        return jnp.einsum('ajb,abk->jk', product.astype(jnp.float32), opm_weight)
    opm_update = lax.map(outer_block, jnp.swapaxes(left_projected_rows, 0, 1))
    pair_mid = (pair_features.astype(jnp.float32) + opm_update).astype(jnp.bfloat16)
    pair_normed = layer_normalize(pair_mid.astype(jnp.float32), 2).astype(jnp.bfloat16)
    logits = jnp.einsum('ijc,ch->hij', pair_normed.astype(jnp.float32), averaging_head_logits.astype(jnp.float32))
    weights = jax.nn.softmax(logits, axis=2).astype(jnp.bfloat16)
    value_rows = jnp.dot(alignment_normalized, averaging_value_weight, preferred_element_type=jnp.float32).astype(jnp.bfloat16)
    value_rows = value_rows.reshape(S, N, HEADS, HDIM)
    averaged = jnp.einsum('hij,sjhd->sihd', weights.astype(jnp.float32), value_rows.astype(jnp.float32)).reshape(S, N, HEADS * HDIM)
    gating_values = jax.nn.sigmoid(jnp.dot(alignment_normalized, averaging_gate_weight, preferred_element_type=jnp.float32))
    gated_output = (gating_values * averaged).astype(jnp.bfloat16)
    alignment_output = (alignment_start.astype(jnp.float32) + jnp.dot(gated_output, averaging_output_weight, preferred_element_type=jnp.float32)).astype(jnp.bfloat16)
    projected = [jnp.dot(pair_normed, triangle_projection_weight[:, column_block * CT:(column_block + 1) * CT], preferred_element_type=jnp.float32) for column_block in range(4)]
    tri_left = (jax.nn.sigmoid(projected[1]) * projected[0]).astype(jnp.bfloat16)
    tri_right = (jax.nn.sigmoid(projected[3]) * projected[2]).astype(jnp.bfloat16)
    tri_sum = jnp.einsum('ikc,jkc->ijc', tri_left.astype(jnp.float32), tri_right.astype(jnp.float32)).astype(jnp.bfloat16)
    tri_normed = layer_normalize(tri_sum.astype(jnp.float32), 2).astype(jnp.bfloat16)
    tri_update = jnp.dot(tri_normed, triangle_output_weight, preferred_element_type=jnp.float32)
    tri_gate = jax.nn.sigmoid(jnp.dot(pair_normed, triangle_gate_weight, preferred_element_type=jnp.float32))
    pair_output = (pair_mid.astype(jnp.float32) + tri_gate * tri_update).astype(jnp.bfloat16)
    return (alignment_output, pair_output)
```

```python
import functools

import jax
import jax.numpy as jnp
from jax import lax
from jax.experimental import pallas as pl
from jax.experimental.pallas import tpu as pltpu
from jax.sharding import PartitionSpec as P


def layer_normalize(inputs, axis):
    average = jnp.mean(inputs, axis=axis, keepdims=True)
    centered = inputs - average
    variance = jnp.mean(centered * centered, axis=axis, keepdims=True)
    return centered * lax.rsqrt(variance + 1e-05)


def local_large(
    alignment_features,
    pair_features,
    token_residue_kind,
    alignment_mask,
    residue_embedding_table,
    outer_left_weight,
    outer_right_weight,
    outer_output_weight,
    averaging_value_weight,
    averaging_gate_weight,
    averaging_head_logits,
    averaging_output_weight,
    triangle_projection_weight,
    triangle_gate_weight,
    triangle_output_weight,
):
    tok_dev = pair_features.shape[0]
    all_tokens = pair_features.shape[1]
    sequences_per_shard = alignment_features.shape[0]
    width = outer_left_weight.shape[1]
    heads = averaging_head_logits.shape[1]
    channels = triangle_output_weight.shape[0]
    classes = residue_embedding_table.shape[0]
    one_hot = (token_residue_kind[:, None] == jnp.arange(classes, dtype=jnp.int32)[None, :]).astype(
        jnp.bfloat16
    )
    embedded_input = jnp.dot(one_hot, residue_embedding_table, preferred_element_type=jnp.float32)
    alignment_start = (alignment_features.astype(jnp.float32) + embedded_input[None]).astype(
        jnp.bfloat16
    )
    alignment_normalized = layer_normalize(alignment_start.astype(jnp.float32), 2).astype(
        jnp.bfloat16
    )
    mask_as_float = alignment_mask.astype(jnp.float32)
    own_mask = lax.dynamic_slice_in_dim(
        mask_as_float, lax.axis_index("row") * sequences_per_shard, sequences_per_shard, 0
    )
    left_projected_rows = (
        jnp.dot(alignment_normalized, outer_left_weight, preferred_element_type=jnp.float32)
        * own_mask[:, None, None]
    ).astype(jnp.bfloat16)
    right_projected_rows = jnp.dot(
        alignment_normalized, outer_right_weight, preferred_element_type=jnp.float32
    ).astype(jnp.bfloat16)
    seq_count = jnp.sum(mask_as_float)
    left_all, right_all = (
        lax.all_gather(left_projected_rows, "row", axis=0, tiled=True),
        lax.all_gather(right_projected_rows, "row", axis=0, tiled=True),
    )
    left_mine = lax.dynamic_slice_in_dim(left_all, lax.axis_index("row") * tok_dev, tok_dev, 1)
    right_flat = right_all.reshape(right_all.shape[0], all_tokens * width)
    opm_weight = outer_output_weight.reshape(width, width, -1)

    def outer_block(left_row):
        summed = jnp.dot(left_row.T, right_flat, preferred_element_type=jnp.float32)
        product = (summed / seq_count).astype(jnp.bfloat16).reshape(width, all_tokens, width)
        return jnp.einsum("ajb,abk->jk", product, opm_weight, preferred_element_type=jnp.float32)

    opm_update = lax.map(outer_block, jnp.swapaxes(left_mine, 0, 1))
    pair_mid = (pair_features.astype(jnp.float32) + opm_update).astype(jnp.bfloat16)
    pair_normed = layer_normalize(pair_mid.astype(jnp.float32), 2).astype(jnp.bfloat16)
    logits = jnp.einsum(
        "ijc,ch->hij", pair_normed, averaging_head_logits, preferred_element_type=jnp.float32
    )
    weights = jax.nn.softmax(logits, axis=2).astype(jnp.bfloat16)
    value_rows = jnp.dot(
        alignment_normalized, averaging_value_weight, preferred_element_type=jnp.float32
    ).astype(jnp.bfloat16)
    value_rows = value_rows.reshape(sequences_per_shard, all_tokens, heads, -1)
    weight_rows = lax.all_gather(weights, "row", axis=1, tiled=True)
    result = jnp.einsum(
        "hij,sjhd->sihd", weight_rows, value_rows, preferred_element_type=jnp.float32
    )
    averaged = result.reshape(sequences_per_shard, weight_rows.shape[1], -1)
    gating_values = jax.nn.sigmoid(
        jnp.dot(alignment_normalized, averaging_gate_weight, preferred_element_type=jnp.float32)
    )
    gated_output = (gating_values * averaged).astype(jnp.bfloat16)
    alignment_output = (
        alignment_start.astype(jnp.float32)
        + jnp.dot(gated_output, averaging_output_weight, preferred_element_type=jnp.float32)
    ).astype(jnp.bfloat16)
    projected = [
        jnp.einsum(
            "ijc,ce->eij",
            pair_normed,
            triangle_projection_weight[:, column_block * channels : (column_block + 1) * channels],
            preferred_element_type=jnp.float32,
        )
        for column_block in range(4)
    ]
    tri_left = (jax.nn.sigmoid(projected[1]) * projected[0]).astype(jnp.bfloat16)
    tri_right = (jax.nn.sigmoid(projected[3]) * projected[2]).astype(jnp.bfloat16)
    owned_left, owned_right = (
        lax.all_to_all(tri_left, "row", split_axis=0, concat_axis=1, tiled=True),
        lax.all_to_all(tri_right, "row", split_axis=0, concat_axis=1, tiled=True),
    )
    tri_sum = jnp.einsum(
        "cik,cjk->cij", owned_left, owned_right, preferred_element_type=jnp.float32
    ).astype(jnp.bfloat16)
    back_rows = lax.all_to_all(tri_sum, "row", split_axis=1, concat_axis=0, tiled=True)
    tri_normed = layer_normalize(back_rows.astype(jnp.float32), 0).astype(jnp.bfloat16)
    tri_update = jnp.einsum(
        "cij,cz->ijz", tri_normed, triangle_output_weight, preferred_element_type=jnp.float32
    )
    tri_gate = jax.nn.sigmoid(
        jnp.dot(pair_normed, triangle_gate_weight, preferred_element_type=jnp.float32)
    )
    pair_output = (pair_mid.astype(jnp.float32) + tri_gate * tri_update).astype(jnp.bfloat16)
    return (alignment_output, pair_output)


F32 = jnp.float32
BF16 = jnp.bfloat16


def matmul(a, b, dim_a, dim_b):
    return lax.dot_general(a, b, (((dim_a,), (dim_b,)), ((), ())), preferred_element_type=F32)


def fused_kernel(
    ranks,
    msa_ref,
    pair_hbm,
    kind_ref,
    mask_ref,
    table_ref,
    left_w_ref,
    right_w_ref,
    outer_w_hbm,
    value_w_ref,
    gate_w_ref,
    head_w_ref,
    average_w_ref,
    tri_w_ref,
    tri_gate_w_ref,
    tri_out_w_ref,
    msa_out_ref,
    pair_out_ref,
    pair_ref,
    outer_w_ref,
    outer_f32,
    left_send,
    left_buf,
    right_buf,
    right_f32,
    right_all,
    left_w_all,
    pair_mid_ref,
    pair_normed_ref,
    weight_buf,
    weight_f32,
    tri_send,
    tri_buf,
    tri_f32,
    back_send,
    back_buf,
    back_f32,
    local_sem,
    send_sem,
    recv_sem,
):
    me = lax.axis_index("row")
    seqs, channels, tokens = msa_ref.shape
    rows = pair_ref.shape[0]
    width = left_w_ref.shape[0]
    heads = head_w_ref.shape[0]
    pair_channels = tri_out_w_ref.shape[1]
    tri_channels = tri_out_w_ref.shape[0]
    owned = tri_channels // ranks
    head_dim = value_w_ref.shape[1] // heads
    sequences = seqs * ranks

    load_pair = pltpu.make_async_copy(pair_hbm, pair_ref, local_sem.at[0])
    load_outer = pltpu.make_async_copy(outer_w_hbm, outer_w_ref, local_sem.at[1])
    load_outer.start()
    load_pair.start()

    barrier = pltpu.get_barrier_semaphore()

    def greet(step, carry):
        pl.semaphore_signal(
            barrier,
            inc=1,
            device_id={"row": lax.rem(me + step, ranks)},
            device_id_type=pl.DeviceIdType.MESH,
        )
        return carry

    lax.fori_loop(1, ranks, greet, 0)

    def remote(phase, step, source, target):
        peer = lax.rem(me + step, ranks)
        return pltpu.make_async_remote_copy(
            src_ref=source.at[peer] if source is not target else source.at[me],
            dst_ref=target.at[me],
            send_sem=send_sem.at[phase, step],
            recv_sem=recv_sem.at[phase, step],
            device_id={"row": peer},
            device_id_type=pl.DeviceIdType.MESH,
        )

    def send_all(phase, source, target):
        def body(step, carry):
            remote(phase, step, source, target).start()
            return carry

        lax.fori_loop(1, ranks, body, 0)

    def receive_all(phase, source, target, wide):
        def body(step, carry):
            remote(phase, step, source, target).wait_recv()
            if wide is not None:
                origin = lax.rem(me - step + ranks, ranks)
                wide[origin] = target[origin].astype(F32).reshape(wide.shape[1:])
            return carry

        lax.fori_loop(1, ranks, body, 0)

    def drain(phase, source, target):
        def body(step, carry):
            remote(phase, step, source, target).wait_send()
            return carry

        lax.fori_loop(1, ranks, body, 0)

    classes = table_ref.shape[0]
    one_hot = jnp.where(
        lax.broadcasted_iota(jnp.int32, (classes, tokens), 0) == kind_ref[...], 1.0, 0.0
    ).astype(BF16)
    embedded = matmul(table_ref[...], one_hot, 0, 0)
    mask = mask_ref[...].astype(F32)
    seq_count = jnp.sum(mask, axis=1, keepdims=True)
    lane = lax.broadcasted_iota(jnp.int32, mask.shape, 1)
    starts = []
    normed = []
    for s in range(seqs):
        start = (msa_ref[s].astype(F32) + embedded).astype(BF16)
        starts.append(start)
        normed.append(layer_normalize(start.astype(F32), 0).astype(BF16))
    msa_normed = jnp.concatenate(normed, axis=1)
    right = matmul(right_w_ref[...], msa_normed, 1, 0).astype(BF16)
    left = matmul(left_w_ref[...], msa_normed, 1, 0)
    left_rows = []
    for s in range(seqs):
        own = jnp.sum(jnp.where(lane == me * seqs + s, mask, 0.0), axis=1, keepdims=True)
        part = slice(s * tokens, (s + 1) * tokens)
        right_buf[me, s * width : (s + 1) * width] = right[:, part]
        left_rows.append((left[:, part] * own).astype(BF16).astype(F32))
    left_rows.append(jnp.zeros((128 - seqs * width, tokens), F32))
    left_turned = jnp.concatenate(left_rows, axis=0).T
    left_send[...] = left_turned.reshape(ranks, rows, 128)

    pl.semaphore_wait(barrier, ranks - 1)
    send_all(0, right_buf, right_buf)
    send_all(1, left_send, left_buf)

    left_buf[me] = left_send[me]
    right_f32[me] = right_buf[me].astype(F32)
    load_outer.wait()
    outer_f32[...] = outer_w_ref[...].astype(F32)
    turned = tri_w_ref[...].astype(F32).T
    blocks = [
        turned[n * tri_channels : (n + 1) * tri_channels].reshape(ranks, owned, pair_channels)
        for n in range(4)
    ]
    project_w = jnp.concatenate([blocks[0], blocks[2]], axis=1).reshape(-1, pair_channels)
    sigmoid_w = jnp.concatenate([blocks[1], blocks[3]], axis=1).reshape(-1, pair_channels)
    tri_w = jnp.concatenate([project_w, sigmoid_w], axis=0).astype(BF16)
    values = matmul(value_w_ref[...], msa_normed, 0, 0).astype(BF16)
    gates = jax.nn.sigmoid(matmul(gate_w_ref[...], msa_normed, 0, 0))

    receive_all(1, left_send, left_buf, None)
    left_lane = lax.broadcasted_iota(jnp.int32, (ranks, seqs * width), 1)
    left_parts = []
    for i in range(rows):
        one = left_buf.reshape(ranks * rows, 128)[pl.ds(i, ranks, stride=rows), :][:, : seqs * width]
        for s in range(seqs):
            keep = (left_lane >= s * width) & (left_lane < (s + 1) * width)
            left_parts.append(jnp.where(keep, one, 0.0))
    left_all = jnp.concatenate(left_parts, axis=0).astype(BF16)
    for b in range(0, width, 2):
        pieces = [
            outer_f32[pl.ds(b + n, width, stride=width), :].astype(BF16) for n in range(2)
        ]
        both = jnp.concatenate(pieces, axis=1)
        product = matmul(left_all, jnp.concatenate([both] * seqs, axis=0), 1, 0).astype(BF16)
        for n in range(2):
            for i in range(rows):
                left_w_all[
                    (b + n) * sequences : (b + n + 1) * sequences,
                    i * pair_channels : (i + 1) * pair_channels,
                ] = product[
                    i * sequences : (i + 1) * sequences,
                    n * pair_channels : (n + 1) * pair_channels,
                ]

    receive_all(0, right_buf, right_buf, right_f32)
    right_flat = right_f32.reshape(ranks * seqs * width, tokens)
    for b in range(width):
        parts = [
            right_flat[pl.ds(s * width + b, ranks, stride=seqs * width), :] for s in range(seqs)
        ]
        right_all[b * sequences : (b + 1) * sequences] = jnp.concatenate(parts, axis=0).astype(BF16)
    load_pair.wait()
    scale = 1.0 / seq_count
    right_turned = right_all[...].T
    for i in range(0, rows, 2):
        update = matmul(
            right_turned, left_w_all[:, i * pair_channels : (i + 2) * pair_channels], 1, 0
        )
        for n in range(2):
            mid = (
                pair_ref[i + n].astype(F32)
                + update[:, n * pair_channels : (n + 1) * pair_channels] * scale
            ).astype(BF16)
            pair_mid_ref[i + n] = mid
            pair_normed_ref[i + n] = layer_normalize(mid.astype(F32), 1).astype(BF16)
        pair_normed = pair_normed_ref[i : i + 2].reshape(2 * tokens, pair_channels)
        projected = matmul(tri_w, pair_normed, 1, 1)
        half = 2 * tri_channels
        gated = (jax.nn.sigmoid(projected[half:]) * projected[:half]).astype(BF16)
        for n in range(2):
            tri_send[:, i + n] = gated[:, n * tokens : (n + 1) * tokens].reshape(
                ranks, 2 * owned, tokens
            )
    send_all(2, tri_send, tri_buf)

    pair_normed = pair_normed_ref[...].reshape(rows * tokens, pair_channels)
    logits = matmul(head_w_ref[...], pair_normed, 1, 1)
    logits = jnp.concatenate(
        [logits[:, i * tokens : (i + 1) * tokens] for i in range(rows)], axis=0
    )
    powers = jnp.exp(logits - jnp.max(logits, axis=1, keepdims=True))
    weight_buf[me] = (powers / jnp.sum(powers, axis=1, keepdims=True)).astype(BF16)
    send_all(3, weight_buf, weight_buf)
    weight_f32[me] = weight_buf[me].astype(F32)
    tri_buf[me] = tri_send[me]
    tri_f32[me] = tri_send[me].astype(F32).reshape(tri_f32.shape[1:])
    tri_gate = jax.nn.sigmoid(matmul(pair_normed, tri_gate_w_ref[...], 1, 0))

    receive_all(2, tri_send, tri_buf, tri_f32)
    tri_flat = tri_f32.reshape(ranks * rows * 2 * owned, tokens)
    sums = []
    for c in range(owned):
        sides = [
            tri_flat[pl.ds(n * owned + c, tokens, stride=2 * owned), :].astype(BF16)
            for n in range(2)
        ]
        sums.append(matmul(sides[0], sides[1], 1, 1).reshape(ranks, rows, tokens))
        if c % 2 == 1:
            back_send[:, (c - 1) * rows : (c + 1) * rows] = jnp.concatenate(
                sums[-2:], axis=1
            ).astype(BF16)
    send_all(4, back_send, back_buf)
    back_buf[me] = back_send[me]
    back_f32[me] = back_send[me].astype(F32)

    receive_all(3, weight_buf, weight_buf, weight_f32)
    weight_flat = weight_f32.reshape(ranks * rows * heads, tokens)
    averaged = [[] for _ in range(seqs)]
    for h in range(heads):
        weights = weight_flat[pl.ds(h, tokens, stride=heads), :].astype(BF16)
        part = values[h * head_dim : (h + 1) * head_dim]
        part = jnp.concatenate(
            [part[:, s * tokens : (s + 1) * tokens] for s in range(seqs)], axis=0
        )
        result = matmul(part, weights, 1, 1)
        for s in range(seqs):
            averaged[s].append(result[s * head_dim : (s + 1) * head_dim])
    gated = (
        gates
        * jnp.concatenate([jnp.concatenate(one, axis=0) for one in averaged], axis=1)
    ).astype(BF16)
    update = matmul(average_w_ref[...], gated, 1, 0)
    for s in range(seqs):
        msa_out_ref[s] = (
            starts[s].astype(F32) + update[:, s * tokens : (s + 1) * tokens]
        ).astype(BF16)

    receive_all(4, back_send, back_buf, back_f32)
    back_flat = back_f32.reshape(tri_channels * rows, tokens)
    for i in range(rows):
        one = back_flat[pl.ds(i, tri_channels, stride=rows), :]
        tri_normed = layer_normalize(one, 0).astype(BF16)
        update = matmul(tri_normed, tri_out_w_ref[...], 0, 0)
        pair_out_ref[i] = (
            pair_mid_ref[i].astype(F32) + tri_gate[i * tokens : (i + 1) * tokens] * update
        ).astype(BF16)
    drain(0, right_buf, right_buf)
    drain(1, left_send, left_buf)
    drain(2, tri_send, tri_buf)
    drain(3, weight_buf, weight_buf)
    drain(4, back_send, back_buf)


def local(ranks, *arguments):
    (
        alignment_features,
        pair_features,
        token_residue_kind,
        alignment_mask,
        residue_embedding_table,
        outer_left_weight,
        outer_right_weight,
        outer_output_weight,
        averaging_value_weight,
        averaging_gate_weight,
        averaging_head_logits,
        averaging_output_weight,
        triangle_projection_weight,
        triangle_gate_weight,
        triangle_output_weight,
    ) = arguments
    seqs, tokens, channels = alignment_features.shape
    rows, _, pair_channels = pair_features.shape
    tri_channels = triangle_output_weight.shape[0]
    width = outer_left_weight.shape[1]
    heads = averaging_head_logits.shape[1]
    owned = tri_channels // ranks
    if (2 * owned) % 16 or rows != 8 or heads != 8 or (seqs * ranks) % 16 or seqs * width > 128:
        return local_large(*arguments)
    sequences = seqs * ranks
    vmem = pl.BlockSpec(memory_space=pltpu.VMEM)
    hbm = pl.BlockSpec(memory_space=pl.ANY)
    in_specs = [vmem] * 15
    in_specs[1] = hbm
    in_specs[7] = hbm
    msa_out, pair_out = pl.pallas_call(
        functools.partial(fused_kernel, ranks),
        out_shape=(
            jax.ShapeDtypeStruct((seqs, channels, tokens), BF16),
            jax.ShapeDtypeStruct((rows, tokens, pair_channels), BF16),
        ),
        in_specs=in_specs,
        out_specs=(vmem, vmem),
        scratch_shapes=[
            pltpu.VMEM((rows, tokens, pair_channels), BF16),
            pltpu.VMEM((width * width, pair_channels), BF16),
            pltpu.VMEM((width * width, pair_channels), F32),
            pltpu.VMEM((ranks, rows, 128), F32),
            pltpu.VMEM((ranks, rows, 128), F32),
            pltpu.VMEM((ranks, seqs * width, tokens), BF16),
            pltpu.VMEM((ranks, seqs * width, tokens), F32),
            pltpu.VMEM((width * sequences, tokens), BF16),
            pltpu.VMEM((width * sequences, rows * pair_channels), BF16),
            pltpu.VMEM((rows, tokens, pair_channels), BF16),
            pltpu.VMEM((rows, tokens, pair_channels), BF16),
            pltpu.VMEM((ranks, rows * heads, tokens), BF16),
            pltpu.VMEM((ranks, rows * heads, tokens), F32),
            pltpu.VMEM((ranks, rows, 2 * owned, tokens), BF16),
            pltpu.VMEM((ranks, rows, 2 * owned, tokens), BF16),
            pltpu.VMEM((ranks, rows * 2 * owned, tokens), F32),
            pltpu.VMEM((ranks, owned * rows, tokens), BF16),
            pltpu.VMEM((ranks, owned * rows, tokens), BF16),
            pltpu.VMEM((ranks, owned * rows, tokens), F32),
            pltpu.SemaphoreType.DMA((2,)),
            pltpu.SemaphoreType.DMA((5, ranks)),
            pltpu.SemaphoreType.DMA((5, ranks)),
        ],
        compiler_params=pltpu.CompilerParams(
            collective_id=0, has_side_effects=True, vmem_limit_bytes=40 * 2**20
        ),
    )(
        jnp.swapaxes(alignment_features, 1, 2),
        pair_features,
        token_residue_kind.reshape(1, tokens),
        alignment_mask.reshape(1, sequences),
        residue_embedding_table,
        outer_left_weight.T,
        outer_right_weight.T,
        outer_output_weight,
        averaging_value_weight,
        averaging_gate_weight,
        averaging_head_logits.T,
        averaging_output_weight.T,
        triangle_projection_weight,
        triangle_gate_weight,
        triangle_output_weight,
    )
    return jnp.swapaxes(msa_out, 1, 2), pair_out


def solution(mesh):
    placed = (
        P(("groups", "row"), None, None),
        P(("groups", "row"), None, None),
        P("groups"),
        P("groups"),
        P(),
        P(),
        P(),
        P(),
        P(),
        P(),
        P(),
        P(),
        P(),
        P(),
        P(),
    )
    return jax.shard_map(
        functools.partial(local, mesh.shape["row"]),
        mesh=mesh,
        in_specs=placed,
        out_specs=(P(("groups", "row"), None, None), P(("groups", "row"), None, None)),
        check_vma=False,
    )
```

```python
import functools

import jax
import jax.numpy as jnp
from jax import lax
from jax.experimental import pallas as pl
from jax.experimental.pallas import tpu as pltpu
from jax.sharding import PartitionSpec as P


def layer_normalize(inputs, axis):
    average = jnp.mean(inputs, axis=axis, keepdims=True)
    centered = inputs - average
    variance = jnp.mean(centered * centered, axis=axis, keepdims=True)
    return centered * lax.rsqrt(variance + 1e-05)


def local_large(
    alignment_features,
    pair_features,
    token_residue_kind,
    alignment_mask,
    residue_embedding_table,
    outer_left_weight,
    outer_right_weight,
    outer_output_weight,
    averaging_value_weight,
    averaging_gate_weight,
    averaging_head_logits,
    averaging_output_weight,
    triangle_projection_weight,
    triangle_gate_weight,
    triangle_output_weight,
):
    tok_dev = pair_features.shape[0]
    all_tokens = pair_features.shape[1]
    sequences_per_shard = alignment_features.shape[0]
    width = outer_left_weight.shape[1]
    heads = averaging_head_logits.shape[1]
    channels = triangle_output_weight.shape[0]
    classes = residue_embedding_table.shape[0]
    one_hot = (token_residue_kind[:, None] == jnp.arange(classes, dtype=jnp.int32)[None, :]).astype(
        jnp.bfloat16
    )
    embedded_input = jnp.dot(one_hot, residue_embedding_table, preferred_element_type=jnp.float32)
    alignment_start = (alignment_features.astype(jnp.float32) + embedded_input[None]).astype(
        jnp.bfloat16
    )
    alignment_normalized = layer_normalize(alignment_start.astype(jnp.float32), 2).astype(
        jnp.bfloat16
    )
    mask_as_float = alignment_mask.astype(jnp.float32)
    own_mask = lax.dynamic_slice_in_dim(
        mask_as_float, lax.axis_index("row") * sequences_per_shard, sequences_per_shard, 0
    )
    left_projected_rows = (
        jnp.dot(alignment_normalized, outer_left_weight, preferred_element_type=jnp.float32)
        * own_mask[:, None, None]
    ).astype(jnp.bfloat16)
    right_projected_rows = jnp.dot(
        alignment_normalized, outer_right_weight, preferred_element_type=jnp.float32
    ).astype(jnp.bfloat16)
    seq_count = jnp.sum(mask_as_float)
    left_all, right_all = (
        lax.all_gather(left_projected_rows, "row", axis=0, tiled=True),
        lax.all_gather(right_projected_rows, "row", axis=0, tiled=True),
    )
    left_mine = lax.dynamic_slice_in_dim(left_all, lax.axis_index("row") * tok_dev, tok_dev, 1)
    right_flat = right_all.reshape(right_all.shape[0], all_tokens * width)
    opm_weight = outer_output_weight.reshape(width, width, -1)

    def outer_block(left_row):
        summed = jnp.dot(left_row.T, right_flat, preferred_element_type=jnp.float32)
        product = (summed / seq_count).astype(jnp.bfloat16).reshape(width, all_tokens, width)
        return jnp.einsum("ajb,abk->jk", product, opm_weight, preferred_element_type=jnp.float32)

    opm_update = lax.map(outer_block, jnp.swapaxes(left_mine, 0, 1))
    pair_mid = (pair_features.astype(jnp.float32) + opm_update).astype(jnp.bfloat16)
    pair_normed = layer_normalize(pair_mid.astype(jnp.float32), 2).astype(jnp.bfloat16)
    logits = jnp.einsum(
        "ijc,ch->hij", pair_normed, averaging_head_logits, preferred_element_type=jnp.float32
    )
    weights = jax.nn.softmax(logits, axis=2).astype(jnp.bfloat16)
    value_rows = jnp.dot(
        alignment_normalized, averaging_value_weight, preferred_element_type=jnp.float32
    ).astype(jnp.bfloat16)
    value_rows = value_rows.reshape(sequences_per_shard, all_tokens, heads, -1)
    weight_rows = lax.all_gather(weights, "row", axis=1, tiled=True)
    result = jnp.einsum(
        "hij,sjhd->sihd", weight_rows, value_rows, preferred_element_type=jnp.float32
    )
    averaged = result.reshape(sequences_per_shard, weight_rows.shape[1], -1)
    gating_values = jax.nn.sigmoid(
        jnp.dot(alignment_normalized, averaging_gate_weight, preferred_element_type=jnp.float32)
    )
    gated_output = (gating_values * averaged).astype(jnp.bfloat16)
    alignment_output = (
        alignment_start.astype(jnp.float32)
        + jnp.dot(gated_output, averaging_output_weight, preferred_element_type=jnp.float32)
    ).astype(jnp.bfloat16)
    projected = [
        jnp.einsum(
            "ijc,ce->eij",
            pair_normed,
            triangle_projection_weight[:, column_block * channels : (column_block + 1) * channels],
            preferred_element_type=jnp.float32,
        )
        for column_block in range(4)
    ]
    tri_left = (jax.nn.sigmoid(projected[1]) * projected[0]).astype(jnp.bfloat16)
    tri_right = (jax.nn.sigmoid(projected[3]) * projected[2]).astype(jnp.bfloat16)
    owned_left, owned_right = (
        lax.all_to_all(tri_left, "row", split_axis=0, concat_axis=1, tiled=True),
        lax.all_to_all(tri_right, "row", split_axis=0, concat_axis=1, tiled=True),
    )
    tri_sum = jnp.einsum(
        "cik,cjk->cij", owned_left, owned_right, preferred_element_type=jnp.float32
    ).astype(jnp.bfloat16)
    back_rows = lax.all_to_all(tri_sum, "row", split_axis=1, concat_axis=0, tiled=True)
    tri_normed = layer_normalize(back_rows.astype(jnp.float32), 0).astype(jnp.bfloat16)
    tri_update = jnp.einsum(
        "cij,cz->ijz", tri_normed, triangle_output_weight, preferred_element_type=jnp.float32
    )
    tri_gate = jax.nn.sigmoid(
        jnp.dot(pair_normed, triangle_gate_weight, preferred_element_type=jnp.float32)
    )
    pair_output = (pair_mid.astype(jnp.float32) + tri_gate * tri_update).astype(jnp.bfloat16)
    return (alignment_output, pair_output)


F32 = jnp.float32
BF16 = jnp.bfloat16
PLANE = 4
CHUNK = 2


def matmul(a, b, dim_a, dim_b):
    return lax.dot_general(a, b, (((dim_a,), (dim_b,)), ((), ())), preferred_element_type=F32)


def fused_kernel(
    ranks,
    msa_hbm,
    pair_hbm,
    kind_hbm,
    mask_hbm,
    table_hbm,
    left_w_hbm,
    right_w_hbm,
    outer_w_hbm,
    value_w_hbm,
    gate_w_hbm,
    head_w_hbm,
    average_w_hbm,
    tri_w_hbm,
    tri_gate_w_hbm,
    tri_out_w_hbm,
    msa_out_ref,
    pair_out_ref,
    msa_ref,
    pair_ref,
    kind_ref,
    mask_ref,
    table_ref,
    left_w_ref,
    right_w_ref,
    outer_w_ref,
    value_w_ref,
    gate_w_ref,
    head_w_ref,
    average_w_ref,
    tri_w_ref,
    tri_gate_w_ref,
    tri_out_w_ref,
    outer_f32,
    left_send,
    left_buf,
    right_buf,
    right_f32,
    right_all,
    left_w_all,
    pair_mid_ref,
    pair_normed_ref,
    weight_buf,
    weight_f32,
    tri_send,
    tri_buf,
    tri_f32,
    back_send,
    back_buf,
    back_f32,
    local_sem,
    send_sem,
    recv_sem,
):
    me = lax.axis_index("row")
    seqs, channels, tokens = msa_ref.shape
    rows = pair_ref.shape[0]
    width = left_w_ref.shape[0]
    heads = head_w_ref.shape[0]
    pair_channels = tri_out_w_ref.shape[1]
    tri_channels = tri_out_w_ref.shape[0]
    owned = tri_channels // ranks
    head_dim = value_w_ref.shape[1] // heads
    sequences = seqs * ranks

    sources = (
        msa_hbm,
        pair_hbm,
        kind_hbm,
        mask_hbm,
        table_hbm,
        left_w_hbm,
        right_w_hbm,
        outer_w_hbm,
        value_w_hbm,
        gate_w_hbm,
        head_w_hbm,
        average_w_hbm,
        tri_w_hbm,
        tri_gate_w_hbm,
        tri_out_w_hbm,
    )
    targets = (
        msa_ref,
        pair_ref,
        kind_ref,
        mask_ref,
        table_ref,
        left_w_ref,
        right_w_ref,
        outer_w_ref,
        value_w_ref,
        gate_w_ref,
        head_w_ref,
        average_w_ref,
        tri_w_ref,
        tri_gate_w_ref,
        tri_out_w_ref,
    )
    loads = [
        pltpu.make_async_copy(source, target, local_sem.at[n])
        for n, (source, target) in enumerate(zip(sources, targets))
    ]
    for n in (0, 2, 3, 4, 5, 6, 7, 12, 8, 9, 1, 10, 11, 13, 14):
        loads[n].start()

    barrier = pltpu.get_barrier_semaphore()

    def greet(step, carry):
        pl.semaphore_signal(
            barrier,
            inc=1,
            device_id={"row": lax.rem(me + step, ranks)},
            device_id_type=pl.DeviceIdType.MESH,
        )
        return carry

    lax.fori_loop(1, ranks, greet, 0)

    def exchange(phase, step, source, target):
        peer = lax.rem(me + step, ranks)
        return pltpu.make_async_remote_copy(
            src_ref=source(peer),
            dst_ref=target(me),
            send_sem=send_sem.at[phase, step],
            recv_sem=recv_sem.at[phase, step],
            device_id={"row": peer},
            device_id_type=pl.DeviceIdType.MESH,
        )

    def send_all(phase, source, target):
        def body(step, carry):
            exchange(phase, step, source, target).start()
            return carry

        lax.fori_loop(1, ranks, body, 0)

    def receive_all(phase, source, target, arrived):
        def body(step, carry):
            exchange(phase, step, source, target).wait_recv()
            arrived(lax.rem(me - step + ranks, ranks))
            return carry

        lax.fori_loop(1, ranks, body, 0)

    def drain(phase, source, target):
        def body(step, carry):
            exchange(phase, step, source, target).wait_send()
            return carry

        lax.fori_loop(1, ranks, body, 0)

    planes = ranks // PLANE
    my_plane = me // PLANE
    place = lax.rem(me, PLANE)

    def origin_of(far, near):
        plane = lax.rem(my_plane - far + planes, planes)
        return plane * PLANE + lax.rem(place - near + PLANE, PLANE)

    def gather(phase, far, near, buffer):
        if near == 0:
            peer = lax.rem(my_plane + far, planes) * PLANE + place
            block = me
        else:
            peer = my_plane * PLANE + lax.rem(place + near, PLANE)
            block = origin_of(far, 0)
        return pltpu.make_async_remote_copy(
            src_ref=buffer.at[block],
            dst_ref=buffer.at[block],
            send_sem=send_sem.at[phase, far * PLANE + near],
            recv_sem=recv_sem.at[phase, far * PLANE + near],
            device_id={"row": peer},
            device_id_type=pl.DeviceIdType.MESH,
        )

    def gather_start(phase, buffer):
        for far in range(1, planes):
            gather(phase, far, 0, buffer).start()
        for near in range(1, PLANE):
            gather(phase, 0, near, buffer).start()

    def gather_forward(phase, buffer):
        for far in range(1, planes):
            gather(phase, far, 0, buffer).wait_recv()
            for near in range(1, PLANE):
                gather(phase, far, near, buffer).start()

    def gather_finish(phase, buffer, wide):
        wide[me] = buffer[me].astype(F32)
        for far in range(1, planes):
            wide[origin_of(far, 0)] = buffer[origin_of(far, 0)].astype(F32)
        for far in range(planes):
            for near in range(1, PLANE):
                gather(phase, far, near, buffer).wait_recv()
                wide[origin_of(far, near)] = buffer[origin_of(far, near)].astype(F32)

    def gather_drain(phase, buffer):
        for step in range(1, ranks):
            gather(phase, step // PLANE, step % PLANE, buffer).wait_send()

    def piece(ref, chunk):
        return lambda rank: ref.at[rank, chunk * CHUNK : (chunk + 1) * CHUNK]

    for n in (0, 2, 3, 4, 5, 6):
        loads[n].wait()
    classes = table_ref.shape[0]
    one_hot = jnp.where(
        lax.broadcasted_iota(jnp.int32, (classes, tokens), 0) == kind_ref[...], 1.0, 0.0
    ).astype(BF16)
    embedded = matmul(table_ref[...], one_hot, 0, 0)
    mask = mask_ref[...].astype(F32)
    seq_count = jnp.sum(mask, axis=1, keepdims=True)
    lane = lax.broadcasted_iota(jnp.int32, mask.shape, 1)
    starts = []
    normed = []
    for s in range(seqs):
        start = (msa_ref[s].astype(F32) + embedded).astype(BF16)
        starts.append(start)
        normed.append(layer_normalize(start.astype(F32), 0).astype(BF16))
    msa_normed = jnp.concatenate(normed, axis=1)
    right = matmul(right_w_ref[...], msa_normed, 1, 0).astype(BF16)
    left = matmul(left_w_ref[...], msa_normed, 1, 0)
    left_rows = []
    for s in range(seqs):
        own = jnp.sum(jnp.where(lane == me * seqs + s, mask, 0.0), axis=1, keepdims=True)
        part = slice(s * tokens, (s + 1) * tokens)
        right_buf[me, s * width : (s + 1) * width] = right[:, part]
        left_rows.append((left[:, part] * own).astype(BF16).astype(F32))
    left_rows.append(jnp.zeros((128 - seqs * width, tokens), F32))
    left_turned = jnp.concatenate(left_rows, axis=0).T
    left_send[...] = left_turned.reshape(ranks, rows, 128)

    pl.semaphore_wait(barrier, ranks - 1)
    gather_start(0, right_buf)
    left_refs = (lambda rank: left_send.at[rank], lambda rank: left_buf.at[rank])
    send_all(1, *left_refs)

    left_buf[me] = left_send[me]
    for n in (7, 12, 8, 9):
        loads[n].wait()
    outer_f32[...] = outer_w_ref[...].astype(F32)
    turned = tri_w_ref[...].astype(F32).T
    blocks = [
        turned[n * tri_channels : (n + 1) * tri_channels].reshape(ranks, owned, pair_channels)
        for n in range(4)
    ]
    project_w = jnp.concatenate([blocks[0], blocks[2]], axis=1).reshape(-1, pair_channels)
    sigmoid_w = jnp.concatenate([blocks[1], blocks[3]], axis=1).reshape(-1, pair_channels)
    tri_w = jnp.concatenate([project_w, sigmoid_w], axis=0).astype(BF16)
    values = matmul(value_w_ref[...], msa_normed, 0, 0).astype(BF16)
    gates = jax.nn.sigmoid(matmul(gate_w_ref[...], msa_normed, 0, 0))

    gather_forward(0, right_buf)
    receive_all(1, *left_refs, lambda origin: None)
    left_lane = lax.broadcasted_iota(jnp.int32, (ranks, seqs * width), 1)
    left_parts = []
    for i in range(rows):
        one = left_buf.reshape(ranks * rows, 128)[pl.ds(i, ranks, stride=rows), :][:, : seqs * width]
        for s in range(seqs):
            keep = (left_lane >= s * width) & (left_lane < (s + 1) * width)
            left_parts.append(jnp.where(keep, one, 0.0))
    left_all = jnp.concatenate(left_parts, axis=0).astype(BF16)
    for b in range(0, width, 2):
        pieces = [
            outer_f32[pl.ds(b + n, width, stride=width), :].astype(BF16) for n in range(2)
        ]
        both = jnp.concatenate(pieces, axis=1)
        product = matmul(left_all, jnp.concatenate([both] * seqs, axis=0), 1, 0).astype(BF16)
        for n in range(2):
            for i in range(rows):
                left_w_all[
                    (b + n) * sequences : (b + n + 1) * sequences,
                    i * pair_channels : (i + 1) * pair_channels,
                ] = product[
                    i * sequences : (i + 1) * sequences,
                    n * pair_channels : (n + 1) * pair_channels,
                ]

    gather_finish(0, right_buf, right_f32)
    right_flat = right_f32.reshape(ranks * seqs * width, tokens)
    for b in range(width):
        parts = [
            right_flat[pl.ds(s * width + b, ranks, stride=seqs * width), :] for s in range(seqs)
        ]
        right_all[b * sequences : (b + 1) * sequences] = jnp.concatenate(parts, axis=0).astype(BF16)
    for n in (1, 10, 11, 13, 14):
        loads[n].wait()
    scale = 1.0 / seq_count
    right_turned = right_all[...].T
    for i in range(0, rows, 2):
        update = matmul(
            right_turned, left_w_all[:, i * pair_channels : (i + 2) * pair_channels], 1, 0
        )
        for n in range(2):
            mid = (
                pair_ref[i + n].astype(F32)
                + update[:, n * pair_channels : (n + 1) * pair_channels] * scale
            ).astype(BF16)
            pair_mid_ref[i + n] = mid
            pair_normed_ref[i + n] = layer_normalize(mid.astype(F32), 1).astype(BF16)
        pair_normed = pair_normed_ref[i : i + 2].reshape(2 * tokens, pair_channels)
        projected = matmul(tri_w, pair_normed, 1, 1)
        half = 2 * tri_channels
        gated = (jax.nn.sigmoid(projected[half:]) * projected[:half]).astype(BF16)
        for n in range(2):
            tri_send[:, i + n] = gated[:, n * tokens : (n + 1) * tokens].reshape(
                ranks, 2 * owned, tokens
            )
        chunk = i // CHUNK
        send_all(2 + chunk, piece(tri_send, chunk), piece(tri_buf, chunk))

    last = 2 + rows // CHUNK - 1
    pair_normed = pair_normed_ref[...].reshape(rows * tokens, pair_channels)
    logits = matmul(head_w_ref[...], pair_normed, 1, 1)
    logits = jnp.concatenate(
        [logits[:, i * tokens : (i + 1) * tokens] for i in range(rows)], axis=0
    )
    powers = jnp.exp(logits - jnp.max(logits, axis=1, keepdims=True))
    weight_buf[me] = (powers / jnp.sum(powers, axis=1, keepdims=True)).astype(BF16)
    gather_start(1 + last, weight_buf)
    tri_f32[me] = tri_send[me].astype(F32).reshape(tri_f32.shape[1:])
    tri_gate = jax.nn.sigmoid(matmul(pair_normed, tri_gate_w_ref[...], 1, 0))

    for chunk in range(rows // CHUNK):
        part = 2 * owned * CHUNK

        def widen(origin, chunk=chunk, part=part):
            tri_f32[origin, chunk * part : (chunk + 1) * part] = (
                tri_buf[origin, chunk * CHUNK : (chunk + 1) * CHUNK]
                .astype(F32)
                .reshape(part, tokens)
            )

        receive_all(2 + chunk, piece(tri_send, chunk), piece(tri_buf, chunk), widen)
    tri_flat = tri_f32.reshape(ranks * rows * 2 * owned, tokens)
    sums = []
    for c in range(owned):
        sides = [
            tri_flat[pl.ds(n * owned + c, tokens, stride=2 * owned), :].astype(BF16)
            for n in range(2)
        ]
        sums.append(matmul(sides[0], sides[1], 1, 1).reshape(ranks, rows, tokens))
        if c % 2 == 1:
            back_send[:, (c - 1) * rows : (c + 1) * rows] = jnp.concatenate(
                sums[-2:], axis=1
            ).astype(BF16)
    back = (lambda rank: back_send.at[rank], lambda rank: back_buf.at[rank])
    send_all(2 + last, *back)
    gather_forward(1 + last, weight_buf)
    back_f32[me] = back_send[me].astype(F32)

    gather_finish(1 + last, weight_buf, weight_f32)
    weight_flat = weight_f32.reshape(ranks * rows * heads, tokens)
    averaged = [[] for _ in range(seqs)]
    for h in range(heads):
        weights = weight_flat[pl.ds(h, tokens, stride=heads), :].astype(BF16)
        part = values[h * head_dim : (h + 1) * head_dim]
        part = jnp.concatenate(
            [part[:, s * tokens : (s + 1) * tokens] for s in range(seqs)], axis=0
        )
        result = matmul(part, weights, 1, 1)
        for s in range(seqs):
            averaged[s].append(result[s * head_dim : (s + 1) * head_dim])
    gated = (
        gates
        * jnp.concatenate([jnp.concatenate(one, axis=0) for one in averaged], axis=1)
    ).astype(BF16)
    update = matmul(average_w_ref[...], gated, 1, 0)
    for s in range(seqs):
        msa_out_ref[s] = (
            starts[s].astype(F32) + update[:, s * tokens : (s + 1) * tokens]
        ).astype(BF16)


    def widen_back(origin):
        back_f32[origin] = back_buf[origin].astype(F32)

    receive_all(2 + last, *back, widen_back)
    back_flat = back_f32.reshape(tri_channels * rows, tokens)
    for i in range(rows):
        one = back_flat[pl.ds(i, tri_channels, stride=rows), :]
        tri_normed = layer_normalize(one, 0).astype(BF16)
        update = matmul(tri_normed, tri_out_w_ref[...], 0, 0)
        pair_out_ref[i] = (
            pair_mid_ref[i].astype(F32) + tri_gate[i * tokens : (i + 1) * tokens] * update
        ).astype(BF16)
    gather_drain(0, right_buf)
    drain(1, *left_refs)
    for chunk in range(rows // CHUNK):
        drain(2 + chunk, piece(tri_send, chunk), piece(tri_buf, chunk))
    gather_drain(1 + last, weight_buf)
    drain(2 + last, *back)


def local(ranks, *arguments):
    (
        alignment_features,
        pair_features,
        token_residue_kind,
        alignment_mask,
        residue_embedding_table,
        outer_left_weight,
        outer_right_weight,
        outer_output_weight,
        averaging_value_weight,
        averaging_gate_weight,
        averaging_head_logits,
        averaging_output_weight,
        triangle_projection_weight,
        triangle_gate_weight,
        triangle_output_weight,
    ) = arguments
    seqs, tokens, channels = alignment_features.shape
    rows, _, pair_channels = pair_features.shape
    tri_channels = triangle_output_weight.shape[0]
    width = outer_left_weight.shape[1]
    heads = averaging_head_logits.shape[1]
    owned = tri_channels // ranks
    if (2 * owned) % 16 or rows != 8 or heads != 8 or (seqs * ranks) % 16 or seqs * width > 128 or ranks % PLANE:
        return local_large(*arguments)
    sequences = seqs * ranks
    vmem = pl.BlockSpec(memory_space=pltpu.VMEM)
    operands = (
        jnp.swapaxes(alignment_features, 1, 2),
        pair_features,
        token_residue_kind.reshape(1, tokens),
        alignment_mask.reshape(1, sequences),
        residue_embedding_table,
        outer_left_weight.T,
        outer_right_weight.T,
        outer_output_weight,
        averaging_value_weight,
        averaging_gate_weight,
        averaging_head_logits.T,
        averaging_output_weight.T,
        triangle_projection_weight,
        triangle_gate_weight,
        triangle_output_weight,
    )
    msa_out, pair_out = pl.pallas_call(
        functools.partial(fused_kernel, ranks),
        out_shape=(
            jax.ShapeDtypeStruct((seqs, channels, tokens), BF16),
            jax.ShapeDtypeStruct((rows, tokens, pair_channels), BF16),
        ),
        in_specs=[pl.BlockSpec(memory_space=pl.ANY)] * len(operands),
        out_specs=(vmem, vmem),
        scratch_shapes=[
            *[pltpu.VMEM(operand.shape, operand.dtype) for operand in operands],
            pltpu.VMEM((width * width, pair_channels), F32),
            pltpu.VMEM((ranks, rows, 128), F32),
            pltpu.VMEM((ranks, rows, 128), F32),
            pltpu.VMEM((ranks, seqs * width, tokens), BF16),
            pltpu.VMEM((ranks, seqs * width, tokens), F32),
            pltpu.VMEM((width * sequences, tokens), BF16),
            pltpu.VMEM((width * sequences, rows * pair_channels), BF16),
            pltpu.VMEM((rows, tokens, pair_channels), BF16),
            pltpu.VMEM((rows, tokens, pair_channels), BF16),
            pltpu.VMEM((ranks, rows * heads, tokens), BF16),
            pltpu.VMEM((ranks, rows * heads, tokens), F32),
            pltpu.VMEM((ranks, rows, 2 * owned, tokens), BF16),
            pltpu.VMEM((ranks, rows, 2 * owned, tokens), BF16),
            pltpu.VMEM((ranks, rows * 2 * owned, tokens), F32),
            pltpu.VMEM((ranks, owned * rows, tokens), BF16),
            pltpu.VMEM((ranks, owned * rows, tokens), BF16),
            pltpu.VMEM((ranks, owned * rows, tokens), F32),
            pltpu.SemaphoreType.DMA((len(operands),)),
            pltpu.SemaphoreType.DMA((4 + rows // CHUNK, ranks)),
            pltpu.SemaphoreType.DMA((4 + rows // CHUNK, ranks)),
        ],
        compiler_params=pltpu.CompilerParams(
            collective_id=0, has_side_effects=True, vmem_limit_bytes=60 * 2**20
        ),
    )(*operands)
    return jnp.swapaxes(msa_out, 1, 2), pair_out


def solution(mesh):
    placed = (
        P(("groups", "row"), None, None),
        P(("groups", "row"), None, None),
        P("groups"),
        P("groups"),
        P(),
        P(),
        P(),
        P(),
        P(),
        P(),
        P(),
        P(),
        P(),
        P(),
        P(),
    )
    return jax.shard_map(
        functools.partial(local, mesh.shape["row"]),
        mesh=mesh,
        in_specs=placed,
        out_specs=(P(("groups", "row"), None, None), P(("groups", "row"), None, None)),
        check_vma=False,
    )
```

```python
import functools

import jax
import jax.numpy as jnp
from jax import lax
from jax.experimental import pallas as pl
from jax.experimental.pallas import tpu as pltpu
from jax.sharding import PartitionSpec as P


def layer_normalize(inputs, axis):
    average = jnp.mean(inputs, axis=axis, keepdims=True)
    centered = inputs - average
    variance = jnp.mean(centered * centered, axis=axis, keepdims=True)
    return centered * lax.rsqrt(variance + 1e-05)


def local_large(
    alignment_features,
    pair_features,
    token_residue_kind,
    alignment_mask,
    residue_embedding_table,
    outer_left_weight,
    outer_right_weight,
    outer_output_weight,
    averaging_value_weight,
    averaging_gate_weight,
    averaging_head_logits,
    averaging_output_weight,
    triangle_projection_weight,
    triangle_gate_weight,
    triangle_output_weight,
):
    tok_dev = pair_features.shape[0]
    all_tokens = pair_features.shape[1]
    sequences_per_shard = alignment_features.shape[0]
    width = outer_left_weight.shape[1]
    heads = averaging_head_logits.shape[1]
    channels = triangle_output_weight.shape[0]
    classes = residue_embedding_table.shape[0]
    one_hot = (token_residue_kind[:, None] == jnp.arange(classes, dtype=jnp.int32)[None, :]).astype(
        jnp.bfloat16
    )
    embedded_input = jnp.dot(one_hot, residue_embedding_table, preferred_element_type=jnp.float32)
    alignment_start = (alignment_features.astype(jnp.float32) + embedded_input[None]).astype(
        jnp.bfloat16
    )
    alignment_normalized = layer_normalize(alignment_start.astype(jnp.float32), 2).astype(
        jnp.bfloat16
    )
    mask_as_float = alignment_mask.astype(jnp.float32)
    own_mask = lax.dynamic_slice_in_dim(
        mask_as_float, lax.axis_index("row") * sequences_per_shard, sequences_per_shard, 0
    )
    left_projected_rows = (
        jnp.dot(alignment_normalized, outer_left_weight, preferred_element_type=jnp.float32)
        * own_mask[:, None, None]
    ).astype(jnp.bfloat16)
    right_projected_rows = jnp.dot(
        alignment_normalized, outer_right_weight, preferred_element_type=jnp.float32
    ).astype(jnp.bfloat16)
    seq_count = jnp.sum(mask_as_float)
    left_all, right_all = (
        lax.all_gather(left_projected_rows, "row", axis=0, tiled=True),
        lax.all_gather(right_projected_rows, "row", axis=0, tiled=True),
    )
    left_mine = lax.dynamic_slice_in_dim(left_all, lax.axis_index("row") * tok_dev, tok_dev, 1)
    right_flat = right_all.reshape(right_all.shape[0], all_tokens * width)
    opm_weight = outer_output_weight.reshape(width, width, -1)

    def outer_block(left_row):
        summed = jnp.dot(left_row.T, right_flat, preferred_element_type=jnp.float32)
        product = (summed / seq_count).astype(jnp.bfloat16).reshape(width, all_tokens, width)
        return jnp.einsum("ajb,abk->jk", product, opm_weight, preferred_element_type=jnp.float32)

    opm_update = lax.map(outer_block, jnp.swapaxes(left_mine, 0, 1))
    pair_mid = (pair_features.astype(jnp.float32) + opm_update).astype(jnp.bfloat16)
    pair_normed = layer_normalize(pair_mid.astype(jnp.float32), 2).astype(jnp.bfloat16)
    logits = jnp.einsum(
        "ijc,ch->hij", pair_normed, averaging_head_logits, preferred_element_type=jnp.float32
    )
    weights = jax.nn.softmax(logits, axis=2).astype(jnp.bfloat16)
    value_rows = jnp.dot(
        alignment_normalized, averaging_value_weight, preferred_element_type=jnp.float32
    ).astype(jnp.bfloat16)
    value_rows = value_rows.reshape(sequences_per_shard, all_tokens, heads, -1)
    weight_rows = lax.all_gather(weights, "row", axis=1, tiled=True)
    result = jnp.einsum(
        "hij,sjhd->sihd", weight_rows, value_rows, preferred_element_type=jnp.float32
    )
    averaged = result.reshape(sequences_per_shard, weight_rows.shape[1], -1)
    gating_values = jax.nn.sigmoid(
        jnp.dot(alignment_normalized, averaging_gate_weight, preferred_element_type=jnp.float32)
    )
    gated_output = (gating_values * averaged).astype(jnp.bfloat16)
    alignment_output = (
        alignment_start.astype(jnp.float32)
        + jnp.dot(gated_output, averaging_output_weight, preferred_element_type=jnp.float32)
    ).astype(jnp.bfloat16)
    projected = [
        jnp.einsum(
            "ijc,ce->eij",
            pair_normed,
            triangle_projection_weight[:, column_block * channels : (column_block + 1) * channels],
            preferred_element_type=jnp.float32,
        )
        for column_block in range(4)
    ]
    tri_left = (jax.nn.sigmoid(projected[1]) * projected[0]).astype(jnp.bfloat16)
    tri_right = (jax.nn.sigmoid(projected[3]) * projected[2]).astype(jnp.bfloat16)
    owned_left, owned_right = (
        lax.all_to_all(tri_left, "row", split_axis=0, concat_axis=1, tiled=True),
        lax.all_to_all(tri_right, "row", split_axis=0, concat_axis=1, tiled=True),
    )
    tri_sum = jnp.einsum(
        "cik,cjk->cij", owned_left, owned_right, preferred_element_type=jnp.float32
    ).astype(jnp.bfloat16)
    back_rows = lax.all_to_all(tri_sum, "row", split_axis=1, concat_axis=0, tiled=True)
    tri_normed = layer_normalize(back_rows.astype(jnp.float32), 0).astype(jnp.bfloat16)
    tri_update = jnp.einsum(
        "cij,cz->ijz", tri_normed, triangle_output_weight, preferred_element_type=jnp.float32
    )
    tri_gate = jax.nn.sigmoid(
        jnp.dot(pair_normed, triangle_gate_weight, preferred_element_type=jnp.float32)
    )
    pair_output = (pair_mid.astype(jnp.float32) + tri_gate * tri_update).astype(jnp.bfloat16)
    return (alignment_output, pair_output)


F32 = jnp.float32
BF16 = jnp.bfloat16
PLANE = 4
CHUNK = 8


def matmul(a, b, dim_a, dim_b):
    return lax.dot_general(a, b, (((dim_a,), (dim_b,)), ((), ())), preferred_element_type=F32)


def fused_kernel(
    ranks,
    msa_hbm,
    pair_hbm,
    kind_hbm,
    mask_hbm,
    table_hbm,
    left_w_hbm,
    right_w_hbm,
    outer_w_hbm,
    value_w_hbm,
    gate_w_hbm,
    head_w_hbm,
    average_w_hbm,
    tri_w_hbm,
    tri_gate_w_hbm,
    tri_out_w_hbm,
    msa_out_ref,
    pair_out_ref,
    msa_ref,
    pair_ref,
    kind_ref,
    mask_ref,
    table_ref,
    left_w_ref,
    right_w_ref,
    outer_w_ref,
    value_w_ref,
    gate_w_ref,
    head_w_ref,
    average_w_ref,
    tri_w_ref,
    tri_gate_w_ref,
    tri_out_w_ref,
    outer_f32,
    left_send,
    left_buf,
    right_buf,
    right_f32,
    right_all,
    left_w_all,
    pair_mid_ref,
    pair_normed_ref,
    weight_buf,
    weight_f32,
    tri_send,
    tri_buf,
    tri_f32,
    back_send,
    back_buf,
    back_f32,
    local_sem,
    send_sem,
    recv_sem,
):
    me = lax.axis_index("row")
    seqs, channels, tokens = msa_ref.shape
    rows = pair_ref.shape[0]
    width = left_w_ref.shape[0]
    heads = head_w_ref.shape[0]
    pair_channels = tri_out_w_ref.shape[1]
    tri_channels = tri_out_w_ref.shape[0]
    owned = tri_channels // ranks
    head_dim = value_w_ref.shape[1] // heads
    sequences = seqs * ranks

    sources = (
        msa_hbm,
        pair_hbm,
        kind_hbm,
        mask_hbm,
        table_hbm,
        left_w_hbm,
        right_w_hbm,
        outer_w_hbm,
        value_w_hbm,
        gate_w_hbm,
        head_w_hbm,
        average_w_hbm,
        tri_w_hbm,
        tri_gate_w_hbm,
        tri_out_w_hbm,
    )
    targets = (
        msa_ref,
        pair_ref,
        kind_ref,
        mask_ref,
        table_ref,
        left_w_ref,
        right_w_ref,
        outer_w_ref,
        value_w_ref,
        gate_w_ref,
        head_w_ref,
        average_w_ref,
        tri_w_ref,
        tri_gate_w_ref,
        tri_out_w_ref,
    )
    loads = [
        pltpu.make_async_copy(source, target, local_sem.at[n])
        for n, (source, target) in enumerate(zip(sources, targets))
    ]
    for n in (0, 2, 3, 4, 5, 6, 7, 12, 8, 9, 1, 10, 11, 13, 14):
        loads[n].start()

    barrier = pltpu.get_barrier_semaphore()

    def greet(step, carry):
        pl.semaphore_signal(
            barrier,
            inc=1,
            device_id={"row": lax.rem(me + step, ranks)},
            device_id_type=pl.DeviceIdType.MESH,
        )
        return carry

    lax.fori_loop(1, ranks, greet, 0)

    def exchange(phase, step, source, target):
        peer = lax.rem(me + step, ranks)
        return pltpu.make_async_remote_copy(
            src_ref=source(peer),
            dst_ref=target(me),
            send_sem=send_sem.at[phase, step],
            recv_sem=recv_sem.at[phase, step],
            device_id={"row": peer},
            device_id_type=pl.DeviceIdType.MESH,
        )

    def send_all(phase, source, target):
        def body(step, carry):
            exchange(phase, step, source, target).start()
            return carry

        lax.fori_loop(1, ranks, body, 0)

    def receive_all(phase, source, target, arrived):
        def body(step, carry):
            exchange(phase, step, source, target).wait_recv()
            arrived(lax.rem(me - step + ranks, ranks))
            return carry

        lax.fori_loop(1, ranks, body, 0)

    def drain(phase, source, target):
        def body(step, carry):
            exchange(phase, step, source, target).wait_send()
            return carry

        lax.fori_loop(1, ranks, body, 0)

    planes = ranks // PLANE
    my_plane = me // PLANE
    place = lax.rem(me, PLANE)

    def origin_of(far, near):
        plane = lax.rem(my_plane - far + planes, planes)
        return plane * PLANE + lax.rem(place - near + PLANE, PLANE)

    def gather(phase, far, near, buffer):
        if near == 0:
            peer = lax.rem(my_plane + far, planes) * PLANE + place
            block = me
        else:
            peer = my_plane * PLANE + lax.rem(place + near, PLANE)
            block = origin_of(far, 0)
        return pltpu.make_async_remote_copy(
            src_ref=buffer.at[block],
            dst_ref=buffer.at[block],
            send_sem=send_sem.at[phase, far * PLANE + near],
            recv_sem=recv_sem.at[phase, far * PLANE + near],
            device_id={"row": peer},
            device_id_type=pl.DeviceIdType.MESH,
        )

    def gather_start(phase, buffer):
        for far in range(1, planes):
            gather(phase, far, 0, buffer).start()
        for near in range(1, PLANE):
            gather(phase, 0, near, buffer).start()

    def gather_forward(phase, buffer):
        for far in range(1, planes):
            gather(phase, far, 0, buffer).wait_recv()
            for near in range(1, PLANE):
                gather(phase, far, near, buffer).start()

    def gather_finish(phase, buffer, wide):
        wide[me] = buffer[me].astype(F32)
        for far in range(1, planes):
            wide[origin_of(far, 0)] = buffer[origin_of(far, 0)].astype(F32)
        for far in range(planes):
            for near in range(1, PLANE):
                gather(phase, far, near, buffer).wait_recv()
                wide[origin_of(far, near)] = buffer[origin_of(far, near)].astype(F32)

    def gather_drain(phase, buffer):
        for step in range(1, ranks):
            gather(phase, step // PLANE, step % PLANE, buffer).wait_send()

    def piece(ref, chunk):
        return lambda rank: ref.at[rank, chunk * CHUNK : (chunk + 1) * CHUNK]

    for n in (0, 2, 3, 4, 5, 6):
        loads[n].wait()
    classes = table_ref.shape[0]
    one_hot = jnp.where(
        lax.broadcasted_iota(jnp.int32, (classes, tokens), 0) == kind_ref[...], 1.0, 0.0
    ).astype(BF16)
    embedded = matmul(table_ref[...], one_hot, 0, 0)
    mask = mask_ref[...].astype(F32)
    seq_count = jnp.sum(mask, axis=1, keepdims=True)
    lane = lax.broadcasted_iota(jnp.int32, mask.shape, 1)
    starts = []
    normed = []
    for s in range(seqs):
        start = (msa_ref[s].astype(F32) + embedded).astype(BF16)
        starts.append(start)
        normed.append(layer_normalize(start.astype(F32), 0).astype(BF16))
    msa_normed = jnp.concatenate(normed, axis=1)
    right = matmul(right_w_ref[...], msa_normed, 1, 0).astype(BF16)
    left = matmul(left_w_ref[...], msa_normed, 1, 0)
    left_rows = []
    for s in range(seqs):
        own = jnp.sum(jnp.where(lane == me * seqs + s, mask, 0.0), axis=1, keepdims=True)
        part = slice(s * tokens, (s + 1) * tokens)
        right_buf[me, s * width : (s + 1) * width] = right[:, part]
        left_rows.append((left[:, part] * own).astype(BF16).astype(F32))
    left_rows.append(jnp.zeros((128 - seqs * width, tokens), F32))
    left_turned = jnp.concatenate(left_rows, axis=0).T
    left_send[...] = left_turned.reshape(ranks, rows, 128)

    pl.semaphore_wait(barrier, ranks - 1)
    gather_start(0, right_buf)
    left_refs = (lambda rank: left_send.at[rank], lambda rank: left_buf.at[rank])
    send_all(1, *left_refs)

    left_buf[me] = left_send[me]
    for n in (7, 12, 8, 9):
        loads[n].wait()
    outer_f32[...] = outer_w_ref[...].astype(F32)
    turned = tri_w_ref[...].astype(F32).T
    blocks = [
        turned[n * tri_channels : (n + 1) * tri_channels].reshape(ranks, owned, pair_channels)
        for n in range(4)
    ]
    project_w = jnp.concatenate([blocks[0], blocks[2]], axis=1).reshape(-1, pair_channels)
    sigmoid_w = jnp.concatenate([blocks[1], blocks[3]], axis=1).reshape(-1, pair_channels)
    tri_w = jnp.concatenate([project_w, sigmoid_w], axis=0).astype(BF16)
    values = matmul(value_w_ref[...], msa_normed, 0, 0).astype(BF16)
    gates = jax.nn.sigmoid(matmul(gate_w_ref[...], msa_normed, 0, 0))

    gather_forward(0, right_buf)
    receive_all(1, *left_refs, lambda origin: None)
    left_lane = lax.broadcasted_iota(jnp.int32, (ranks, seqs * width), 1)
    left_parts = []
    for i in range(rows):
        one = left_buf.reshape(ranks * rows, 128)[pl.ds(i, ranks, stride=rows), :][:, : seqs * width]
        for s in range(seqs):
            keep = (left_lane >= s * width) & (left_lane < (s + 1) * width)
            left_parts.append(jnp.where(keep, one, 0.0))
    left_all = jnp.concatenate(left_parts, axis=0).astype(BF16)
    for b in range(0, width, 2):
        pieces = [
            outer_f32[pl.ds(b + n, width, stride=width), :].astype(BF16) for n in range(2)
        ]
        both = jnp.concatenate(pieces, axis=1)
        product = matmul(left_all, jnp.concatenate([both] * seqs, axis=0), 1, 0).astype(BF16)
        for n in range(2):
            for i in range(rows):
                left_w_all[
                    (b + n) * sequences : (b + n + 1) * sequences,
                    i * pair_channels : (i + 1) * pair_channels,
                ] = product[
                    i * sequences : (i + 1) * sequences,
                    n * pair_channels : (n + 1) * pair_channels,
                ]

    gather_finish(0, right_buf, right_f32)
    right_flat = right_f32.reshape(ranks * seqs * width, tokens)
    for b in range(width):
        parts = [
            right_flat[pl.ds(s * width + b, ranks, stride=seqs * width), :] for s in range(seqs)
        ]
        right_all[b * sequences : (b + 1) * sequences] = jnp.concatenate(parts, axis=0).astype(BF16)
    for n in (1, 10, 11, 13, 14):
        loads[n].wait()
    scale = 1.0 / seq_count
    right_turned = right_all[...].T
    for i in range(0, rows, 2):
        update = matmul(
            right_turned, left_w_all[:, i * pair_channels : (i + 2) * pair_channels], 1, 0
        )
        for n in range(2):
            mid = (
                pair_ref[i + n].astype(F32)
                + update[:, n * pair_channels : (n + 1) * pair_channels] * scale
            ).astype(BF16)
            pair_mid_ref[i + n] = mid
            pair_normed_ref[i + n] = layer_normalize(mid.astype(F32), 1).astype(BF16)
        pair_normed = pair_normed_ref[i : i + 2].reshape(2 * tokens, pair_channels)
        projected = matmul(tri_w, pair_normed, 1, 1)
        half = 2 * tri_channels
        gated = (jax.nn.sigmoid(projected[half:]) * projected[:half]).astype(BF16)
        for n in range(2):
            tri_send[:, i + n] = gated[:, n * tokens : (n + 1) * tokens].reshape(
                ranks, 2 * owned, tokens
            )
        if (i + 2) % CHUNK == 0:
            chunk = i // CHUNK
            send_all(2 + chunk, piece(tri_send, chunk), piece(tri_buf, chunk))

    last = 2 + rows // CHUNK - 1
    pair_normed = pair_normed_ref[...].reshape(rows * tokens, pair_channels)
    logits = matmul(head_w_ref[...], pair_normed, 1, 1)
    logits = jnp.concatenate(
        [logits[:, i * tokens : (i + 1) * tokens] for i in range(rows)], axis=0
    )
    powers = jnp.exp(logits - jnp.max(logits, axis=1, keepdims=True))
    weight_buf[me] = (powers / jnp.sum(powers, axis=1, keepdims=True)).astype(BF16)
    gather_start(1 + last, weight_buf)
    tri_f32[me] = tri_send[me].astype(F32).reshape(tri_f32.shape[1:])
    tri_gate = jax.nn.sigmoid(matmul(pair_normed, tri_gate_w_ref[...], 1, 0))

    for chunk in range(rows // CHUNK):
        part = 2 * owned * CHUNK

        def widen(origin, chunk=chunk, part=part):
            tri_f32[origin, chunk * part : (chunk + 1) * part] = (
                tri_buf[origin, chunk * CHUNK : (chunk + 1) * CHUNK]
                .astype(F32)
                .reshape(part, tokens)
            )

        receive_all(2 + chunk, piece(tri_send, chunk), piece(tri_buf, chunk), widen)
    tri_flat = tri_f32.reshape(ranks * rows * 2 * owned, tokens)
    sums = []
    for c in range(owned):
        sides = [
            tri_flat[pl.ds(n * owned + c, tokens, stride=2 * owned), :].astype(BF16)
            for n in range(2)
        ]
        sums.append(matmul(sides[0], sides[1], 1, 1).reshape(ranks, rows, tokens))
        if c % 2 == 1:
            back_send[:, (c - 1) * rows : (c + 1) * rows] = jnp.concatenate(
                sums[-2:], axis=1
            ).astype(BF16)
    back = (lambda rank: back_send.at[rank], lambda rank: back_buf.at[rank])
    send_all(2 + last, *back)
    gather_forward(1 + last, weight_buf)
    back_f32[me] = back_send[me].astype(F32)

    gather_finish(1 + last, weight_buf, weight_f32)
    weight_flat = weight_f32.reshape(ranks * rows * heads, tokens)
    averaged = [[] for _ in range(seqs)]
    for h in range(heads):
        weights = weight_flat[pl.ds(h, tokens, stride=heads), :].astype(BF16)
        part = values[h * head_dim : (h + 1) * head_dim]
        part = jnp.concatenate(
            [part[:, s * tokens : (s + 1) * tokens] for s in range(seqs)], axis=0
        )
        result = matmul(part, weights, 1, 1)
        for s in range(seqs):
            averaged[s].append(result[s * head_dim : (s + 1) * head_dim])
    gated = (
        gates
        * jnp.concatenate([jnp.concatenate(one, axis=0) for one in averaged], axis=1)
    ).astype(BF16)
    update = matmul(average_w_ref[...], gated, 1, 0)
    for s in range(seqs):
        msa_out_ref[s] = (
            starts[s].astype(F32) + update[:, s * tokens : (s + 1) * tokens]
        ).astype(BF16)


    def widen_back(origin):
        back_f32[origin] = back_buf[origin].astype(F32)

    receive_all(2 + last, *back, widen_back)
    back_flat = back_f32.reshape(tri_channels * rows, tokens)
    for i in range(rows):
        one = back_flat[pl.ds(i, tri_channels, stride=rows), :]
        tri_normed = layer_normalize(one, 0).astype(BF16)
        update = matmul(tri_normed, tri_out_w_ref[...], 0, 0)
        pair_out_ref[i] = (
            pair_mid_ref[i].astype(F32) + tri_gate[i * tokens : (i + 1) * tokens] * update
        ).astype(BF16)
    gather_drain(0, right_buf)
    drain(1, *left_refs)
    for chunk in range(rows // CHUNK):
        drain(2 + chunk, piece(tri_send, chunk), piece(tri_buf, chunk))
    gather_drain(1 + last, weight_buf)
    drain(2 + last, *back)


def local(ranks, *arguments):
    (
        alignment_features,
        pair_features,
        token_residue_kind,
        alignment_mask,
        residue_embedding_table,
        outer_left_weight,
        outer_right_weight,
        outer_output_weight,
        averaging_value_weight,
        averaging_gate_weight,
        averaging_head_logits,
        averaging_output_weight,
        triangle_projection_weight,
        triangle_gate_weight,
        triangle_output_weight,
    ) = arguments
    seqs, tokens, channels = alignment_features.shape
    rows, _, pair_channels = pair_features.shape
    tri_channels = triangle_output_weight.shape[0]
    width = outer_left_weight.shape[1]
    heads = averaging_head_logits.shape[1]
    owned = tri_channels // ranks
    if (2 * owned) % 16 or rows != 8 or heads != 8 or (seqs * ranks) % 16 or seqs * width > 128 or ranks % PLANE:
        return local_large(*arguments)
    sequences = seqs * ranks
    vmem = pl.BlockSpec(memory_space=pltpu.VMEM)
    operands = (
        jnp.swapaxes(alignment_features, 1, 2),
        pair_features,
        token_residue_kind.reshape(1, tokens),
        alignment_mask.reshape(1, sequences),
        residue_embedding_table,
        outer_left_weight.T,
        outer_right_weight.T,
        outer_output_weight,
        averaging_value_weight,
        averaging_gate_weight,
        averaging_head_logits.T,
        averaging_output_weight.T,
        triangle_projection_weight,
        triangle_gate_weight,
        triangle_output_weight,
    )
    msa_out, pair_out = pl.pallas_call(
        functools.partial(fused_kernel, ranks),
        out_shape=(
            jax.ShapeDtypeStruct((seqs, channels, tokens), BF16),
            jax.ShapeDtypeStruct((rows, tokens, pair_channels), BF16),
        ),
        in_specs=[pl.BlockSpec(memory_space=pl.ANY)] * len(operands),
        out_specs=(vmem, vmem),
        scratch_shapes=[
            *[pltpu.VMEM(operand.shape, operand.dtype) for operand in operands],
            pltpu.VMEM((width * width, pair_channels), F32),
            pltpu.VMEM((ranks, rows, 128), F32),
            pltpu.VMEM((ranks, rows, 128), F32),
            pltpu.VMEM((ranks, seqs * width, tokens), BF16),
            pltpu.VMEM((ranks, seqs * width, tokens), F32),
            pltpu.VMEM((width * sequences, tokens), BF16),
            pltpu.VMEM((width * sequences, rows * pair_channels), BF16),
            pltpu.VMEM((rows, tokens, pair_channels), BF16),
            pltpu.VMEM((rows, tokens, pair_channels), BF16),
            pltpu.VMEM((ranks, rows * heads, tokens), BF16),
            pltpu.VMEM((ranks, rows * heads, tokens), F32),
            pltpu.VMEM((ranks, rows, 2 * owned, tokens), BF16),
            pltpu.VMEM((ranks, rows, 2 * owned, tokens), BF16),
            pltpu.VMEM((ranks, rows * 2 * owned, tokens), F32),
            pltpu.VMEM((ranks, owned * rows, tokens), BF16),
            pltpu.VMEM((ranks, owned * rows, tokens), BF16),
            pltpu.VMEM((ranks, owned * rows, tokens), F32),
            pltpu.SemaphoreType.DMA((len(operands),)),
            pltpu.SemaphoreType.DMA((4 + rows // CHUNK, ranks)),
            pltpu.SemaphoreType.DMA((4 + rows // CHUNK, ranks)),
        ],
        compiler_params=pltpu.CompilerParams(
            collective_id=0, has_side_effects=True, vmem_limit_bytes=60 * 2**20
        ),
    )(*operands)
    return jnp.swapaxes(msa_out, 1, 2), pair_out


def solution(mesh):
    placed = (
        P(("groups", "row"), None, None),
        P(("groups", "row"), None, None),
        P("groups"),
        P("groups"),
        P(),
        P(),
        P(),
        P(),
        P(),
        P(),
        P(),
        P(),
        P(),
        P(),
        P(),
    )
    return jax.shard_map(
        functools.partial(local, mesh.shape["row"]),
        mesh=mesh,
        in_specs=placed,
        out_specs=(P(("groups", "row"), None, None), P(("groups", "row"), None, None)),
        check_vma=False,
    )
```

```python
import functools

import jax
import jax.numpy as jnp
from jax import lax
from jax.experimental import pallas as pl
from jax.experimental.pallas import tpu as pltpu
from jax.sharding import PartitionSpec as P


def layer_normalize(inputs, axis):
    average = jnp.mean(inputs, axis=axis, keepdims=True)
    centered = inputs - average
    variance = jnp.mean(centered * centered, axis=axis, keepdims=True)
    return centered * lax.rsqrt(variance + 1e-05)


def local_large(
    alignment_features,
    pair_features,
    token_residue_kind,
    alignment_mask,
    residue_embedding_table,
    outer_left_weight,
    outer_right_weight,
    outer_output_weight,
    averaging_value_weight,
    averaging_gate_weight,
    averaging_head_logits,
    averaging_output_weight,
    triangle_projection_weight,
    triangle_gate_weight,
    triangle_output_weight,
):
    tok_dev = pair_features.shape[0]
    all_tokens = pair_features.shape[1]
    sequences_per_shard = alignment_features.shape[0]
    width = outer_left_weight.shape[1]
    heads = averaging_head_logits.shape[1]
    channels = triangle_output_weight.shape[0]
    classes = residue_embedding_table.shape[0]
    one_hot = (token_residue_kind[:, None] == jnp.arange(classes, dtype=jnp.int32)[None, :]).astype(
        jnp.bfloat16
    )
    embedded_input = jnp.dot(one_hot, residue_embedding_table, preferred_element_type=jnp.float32)
    alignment_start = (alignment_features.astype(jnp.float32) + embedded_input[None]).astype(
        jnp.bfloat16
    )
    alignment_normalized = layer_normalize(alignment_start.astype(jnp.float32), 2).astype(
        jnp.bfloat16
    )
    mask_as_float = alignment_mask.astype(jnp.float32)
    own_mask = lax.dynamic_slice_in_dim(
        mask_as_float, lax.axis_index("row") * sequences_per_shard, sequences_per_shard, 0
    )
    left_projected_rows = (
        jnp.dot(alignment_normalized, outer_left_weight, preferred_element_type=jnp.float32)
        * own_mask[:, None, None]
    ).astype(jnp.bfloat16)
    right_projected_rows = jnp.dot(
        alignment_normalized, outer_right_weight, preferred_element_type=jnp.float32
    ).astype(jnp.bfloat16)
    seq_count = jnp.sum(mask_as_float)
    left_all, right_all = (
        lax.all_gather(left_projected_rows, "row", axis=0, tiled=True),
        lax.all_gather(right_projected_rows, "row", axis=0, tiled=True),
    )
    left_mine = lax.dynamic_slice_in_dim(left_all, lax.axis_index("row") * tok_dev, tok_dev, 1)
    right_flat = right_all.reshape(right_all.shape[0], all_tokens * width)
    opm_weight = outer_output_weight.reshape(width, width, -1)

    def outer_block(left_row):
        summed = jnp.dot(left_row.T, right_flat, preferred_element_type=jnp.float32)
        product = (summed / seq_count).astype(jnp.bfloat16).reshape(width, all_tokens, width)
        return jnp.einsum("ajb,abk->jk", product, opm_weight, preferred_element_type=jnp.float32)

    opm_update = lax.map(outer_block, jnp.swapaxes(left_mine, 0, 1))
    pair_mid = (pair_features.astype(jnp.float32) + opm_update).astype(jnp.bfloat16)
    pair_normed = layer_normalize(pair_mid.astype(jnp.float32), 2).astype(jnp.bfloat16)
    logits = jnp.einsum(
        "ijc,ch->hij", pair_normed, averaging_head_logits, preferred_element_type=jnp.float32
    )
    weights = jax.nn.softmax(logits, axis=2).astype(jnp.bfloat16)
    value_rows = jnp.dot(
        alignment_normalized, averaging_value_weight, preferred_element_type=jnp.float32
    ).astype(jnp.bfloat16)
    value_rows = value_rows.reshape(sequences_per_shard, all_tokens, heads, -1)
    weight_rows = lax.all_gather(weights, "row", axis=1, tiled=True)
    result = jnp.einsum(
        "hij,sjhd->sihd", weight_rows, value_rows, preferred_element_type=jnp.float32
    )
    averaged = result.reshape(sequences_per_shard, weight_rows.shape[1], -1)
    gating_values = jax.nn.sigmoid(
        jnp.dot(alignment_normalized, averaging_gate_weight, preferred_element_type=jnp.float32)
    )
    gated_output = (gating_values * averaged).astype(jnp.bfloat16)
    alignment_output = (
        alignment_start.astype(jnp.float32)
        + jnp.dot(gated_output, averaging_output_weight, preferred_element_type=jnp.float32)
    ).astype(jnp.bfloat16)
    projected = [
        jnp.einsum(
            "ijc,ce->eij",
            pair_normed,
            triangle_projection_weight[:, column_block * channels : (column_block + 1) * channels],
            preferred_element_type=jnp.float32,
        )
        for column_block in range(4)
    ]
    tri_left = (jax.nn.sigmoid(projected[1]) * projected[0]).astype(jnp.bfloat16)
    tri_right = (jax.nn.sigmoid(projected[3]) * projected[2]).astype(jnp.bfloat16)
    owned_left, owned_right = (
        lax.all_to_all(tri_left, "row", split_axis=0, concat_axis=1, tiled=True),
        lax.all_to_all(tri_right, "row", split_axis=0, concat_axis=1, tiled=True),
    )
    tri_sum = jnp.einsum(
        "cik,cjk->cij", owned_left, owned_right, preferred_element_type=jnp.float32
    ).astype(jnp.bfloat16)
    back_rows = lax.all_to_all(tri_sum, "row", split_axis=1, concat_axis=0, tiled=True)
    tri_normed = layer_normalize(back_rows.astype(jnp.float32), 0).astype(jnp.bfloat16)
    tri_update = jnp.einsum(
        "cij,cz->ijz", tri_normed, triangle_output_weight, preferred_element_type=jnp.float32
    )
    tri_gate = jax.nn.sigmoid(
        jnp.dot(pair_normed, triangle_gate_weight, preferred_element_type=jnp.float32)
    )
    pair_output = (pair_mid.astype(jnp.float32) + tri_gate * tri_update).astype(jnp.bfloat16)
    return (alignment_output, pair_output)


F32 = jnp.float32
BF16 = jnp.bfloat16
PLANE = 4
CHUNK = 8


def matmul(a, b, dim_a, dim_b):
    return lax.dot_general(a, b, (((dim_a,), (dim_b,)), ((), ())), preferred_element_type=F32)


def fused_kernel(
    ranks,
    msa_hbm,
    pair_hbm,
    kind_hbm,
    mask_hbm,
    table_hbm,
    left_w_hbm,
    right_w_hbm,
    outer_w_hbm,
    value_w_hbm,
    gate_w_hbm,
    head_w_hbm,
    average_w_hbm,
    tri_w_hbm,
    tri_gate_w_hbm,
    tri_out_w_hbm,
    msa_out_ref,
    pair_out_ref,
    msa_ref,
    pair_ref,
    kind_ref,
    mask_ref,
    table_ref,
    left_w_ref,
    right_w_ref,
    outer_w_ref,
    value_w_ref,
    gate_w_ref,
    head_w_ref,
    average_w_ref,
    tri_w_ref,
    tri_gate_w_ref,
    tri_out_w_ref,
    outer_f32,
    left_send,
    left_buf,
    right_buf,
    right_f32,
    right_all,
    left_w_all,
    pair_mid_ref,
    pair_normed_ref,
    weight_buf,
    weight_f32,
    tri_send,
    tri_buf,
    tri_f32,
    back_send,
    back_buf,
    back_f32,
    local_sem,
    send_sem,
    recv_sem,
):
    me = lax.axis_index("row")
    seqs, channels, tokens = msa_ref.shape
    rows = pair_ref.shape[0]
    width = left_w_ref.shape[0]
    heads = head_w_ref.shape[0]
    pair_channels = tri_out_w_ref.shape[1]
    tri_channels = tri_out_w_ref.shape[0]
    owned = tri_channels // ranks
    head_dim = value_w_ref.shape[1] // heads
    sequences = seqs * ranks

    sources = (
        msa_hbm,
        pair_hbm,
        kind_hbm,
        mask_hbm,
        table_hbm,
        left_w_hbm,
        right_w_hbm,
        outer_w_hbm,
        value_w_hbm,
        gate_w_hbm,
        head_w_hbm,
        average_w_hbm,
        tri_w_hbm,
        tri_gate_w_hbm,
        tri_out_w_hbm,
    )
    targets = (
        msa_ref,
        pair_ref,
        kind_ref,
        mask_ref,
        table_ref,
        left_w_ref,
        right_w_ref,
        outer_w_ref,
        value_w_ref,
        gate_w_ref,
        head_w_ref,
        average_w_ref,
        tri_w_ref,
        tri_gate_w_ref,
        tri_out_w_ref,
    )
    loads = [
        pltpu.make_async_copy(source, target, local_sem.at[n])
        for n, (source, target) in enumerate(zip(sources, targets))
    ]
    for n in (0, 2, 3, 4, 5, 6, 7, 12, 8, 9, 1, 10, 11, 13, 14):
        loads[n].start()

    barrier = pltpu.get_barrier_semaphore()

    def greet(step, carry):
        pl.semaphore_signal(
            barrier,
            inc=1,
            device_id={"row": lax.rem(me + step, ranks)},
            device_id_type=pl.DeviceIdType.MESH,
        )
        return carry

    lax.fori_loop(1, ranks, greet, 0)

    def exchange(phase, step, source, target):
        peer = lax.rem(me + step, ranks)
        return pltpu.make_async_remote_copy(
            src_ref=source(peer),
            dst_ref=target(me),
            send_sem=send_sem.at[phase, step],
            recv_sem=recv_sem.at[phase, step],
            device_id={"row": peer},
            device_id_type=pl.DeviceIdType.MESH,
        )

    def send_all(phase, source, target):
        def body(step, carry):
            exchange(phase, step, source, target).start()
            return carry

        lax.fori_loop(1, ranks, body, 0, unroll=True)

    def receive_all(phase, source, target, arrived):
        def body(step, carry):
            exchange(phase, step, source, target).wait_recv()
            arrived(lax.rem(me - step + ranks, ranks))
            return carry

        lax.fori_loop(1, ranks, body, 0, unroll=True)

    def drain(phase, source, target):
        def body(step, carry):
            exchange(phase, step, source, target).wait_send()
            return carry

        lax.fori_loop(1, ranks, body, 0, unroll=True)

    planes = ranks // PLANE
    my_plane = me // PLANE
    place = lax.rem(me, PLANE)

    def origin_of(far, near):
        plane = lax.rem(my_plane - far + planes, planes)
        return plane * PLANE + lax.rem(place - near + PLANE, PLANE)

    def gather(phase, far, near, buffer):
        if near == 0:
            peer = lax.rem(my_plane + far, planes) * PLANE + place
            block = me
        else:
            peer = my_plane * PLANE + lax.rem(place + near, PLANE)
            block = origin_of(far, 0)
        return pltpu.make_async_remote_copy(
            src_ref=buffer.at[block],
            dst_ref=buffer.at[block],
            send_sem=send_sem.at[phase, far * PLANE + near],
            recv_sem=recv_sem.at[phase, far * PLANE + near],
            device_id={"row": peer},
            device_id_type=pl.DeviceIdType.MESH,
        )

    def gather_start(phase, buffer):
        for far in range(1, planes):
            gather(phase, far, 0, buffer).start()
        for near in range(1, PLANE):
            gather(phase, 0, near, buffer).start()

    def gather_forward(phase, buffer):
        for far in range(1, planes):
            gather(phase, far, 0, buffer).wait_recv()
            for near in range(1, PLANE):
                gather(phase, far, near, buffer).start()

    def gather_finish(phase, buffer, wide):
        wide[me] = buffer[me].astype(F32)
        for far in range(1, planes):
            wide[origin_of(far, 0)] = buffer[origin_of(far, 0)].astype(F32)
        for far in range(planes):
            for near in range(1, PLANE):
                gather(phase, far, near, buffer).wait_recv()
                wide[origin_of(far, near)] = buffer[origin_of(far, near)].astype(F32)

    def gather_drain(phase, buffer):
        for step in range(1, ranks):
            gather(phase, step // PLANE, step % PLANE, buffer).wait_send()

    def piece(ref, chunk):
        return lambda rank: ref.at[rank, chunk * CHUNK : (chunk + 1) * CHUNK]

    for n in (0, 2, 3, 4, 5, 6):
        loads[n].wait()
    classes = table_ref.shape[0]
    one_hot = jnp.where(
        lax.broadcasted_iota(jnp.int32, (classes, tokens), 0) == kind_ref[...], 1.0, 0.0
    ).astype(BF16)
    embedded = matmul(table_ref[...], one_hot, 0, 0)
    mask = mask_ref[...].astype(F32)
    seq_count = jnp.sum(mask, axis=1, keepdims=True)
    lane = lax.broadcasted_iota(jnp.int32, mask.shape, 1)
    starts = []
    normed = []
    for s in range(seqs):
        start = (msa_ref[s].astype(F32) + embedded).astype(BF16)
        starts.append(start)
        normed.append(layer_normalize(start.astype(F32), 0).astype(BF16))
    msa_normed = jnp.concatenate(normed, axis=1)
    right = matmul(right_w_ref[...], msa_normed, 1, 0).astype(BF16)
    left = matmul(left_w_ref[...], msa_normed, 1, 0)
    left_rows = []
    for s in range(seqs):
        own = jnp.sum(jnp.where(lane == me * seqs + s, mask, 0.0), axis=1, keepdims=True)
        part = slice(s * tokens, (s + 1) * tokens)
        right_buf[me, s * width : (s + 1) * width] = right[:, part]
        left_rows.append((left[:, part] * own).astype(BF16).astype(F32))
    left_rows.append(jnp.zeros((128 - seqs * width, tokens), F32))
    left_turned = jnp.concatenate(left_rows, axis=0).T
    left_send[...] = left_turned.reshape(ranks, rows, 128)

    pl.semaphore_wait(barrier, ranks - 1)
    gather_start(0, right_buf)
    left_refs = (lambda rank: left_send.at[rank], lambda rank: left_buf.at[rank])
    send_all(1, *left_refs)

    left_buf[me] = left_send[me]
    for n in (7, 12, 8, 9):
        loads[n].wait()
    outer_f32[...] = outer_w_ref[...].astype(F32)
    turned = tri_w_ref[...].astype(F32).T
    blocks = [
        turned[n * tri_channels : (n + 1) * tri_channels].reshape(ranks, owned, pair_channels)
        for n in range(4)
    ]
    project_w = jnp.concatenate([blocks[0], blocks[2]], axis=1).reshape(-1, pair_channels)
    sigmoid_w = jnp.concatenate([blocks[1], blocks[3]], axis=1).reshape(-1, pair_channels)
    tri_w = jnp.concatenate([project_w, sigmoid_w], axis=0).astype(BF16)
    values = matmul(value_w_ref[...], msa_normed, 0, 0).astype(BF16)
    gates = jax.nn.sigmoid(matmul(gate_w_ref[...], msa_normed, 0, 0))

    gather_forward(0, right_buf)
    receive_all(1, *left_refs, lambda origin: None)
    left_lane = lax.broadcasted_iota(jnp.int32, (ranks, seqs * width), 1)
    left_parts = []
    for i in range(rows):
        one = left_buf.reshape(ranks * rows, 128)[pl.ds(i, ranks, stride=rows), :][:, : seqs * width]
        for s in range(seqs):
            keep = (left_lane >= s * width) & (left_lane < (s + 1) * width)
            left_parts.append(jnp.where(keep, one, 0.0))
    left_all = jnp.concatenate(left_parts, axis=0).astype(BF16)
    for b in range(0, width, 2):
        pieces = [
            outer_f32[pl.ds(b + n, width, stride=width), :].astype(BF16) for n in range(2)
        ]
        both = jnp.concatenate(pieces, axis=1)
        product = matmul(left_all, jnp.concatenate([both] * seqs, axis=0), 1, 0).astype(BF16)
        for n in range(2):
            for i in range(rows):
                left_w_all[
                    (b + n) * sequences : (b + n + 1) * sequences,
                    i * pair_channels : (i + 1) * pair_channels,
                ] = product[
                    i * sequences : (i + 1) * sequences,
                    n * pair_channels : (n + 1) * pair_channels,
                ]

    gather_finish(0, right_buf, right_f32)
    right_flat = right_f32.reshape(ranks * seqs * width, tokens)
    for b in range(width):
        parts = [
            right_flat[pl.ds(s * width + b, ranks, stride=seqs * width), :] for s in range(seqs)
        ]
        right_all[b * sequences : (b + 1) * sequences] = jnp.concatenate(parts, axis=0).astype(BF16)
    for n in (1, 10, 11, 13, 14):
        loads[n].wait()
    scale = 1.0 / seq_count
    right_turned = right_all[...].T
    for i in range(0, rows, 2):
        update = matmul(
            right_turned, left_w_all[:, i * pair_channels : (i + 2) * pair_channels], 1, 0
        )
        for n in range(2):
            mid = (
                pair_ref[i + n].astype(F32)
                + update[:, n * pair_channels : (n + 1) * pair_channels] * scale
            ).astype(BF16)
            pair_mid_ref[i + n] = mid
            pair_normed_ref[i + n] = layer_normalize(mid.astype(F32), 1).astype(BF16)
        pair_normed = pair_normed_ref[i : i + 2].reshape(2 * tokens, pair_channels)
        projected = matmul(tri_w, pair_normed, 1, 1)
        half = 2 * tri_channels
        gated = (jax.nn.sigmoid(projected[half:]) * projected[:half]).astype(BF16)
        for n in range(2):
            tri_send[:, i + n] = gated[:, n * tokens : (n + 1) * tokens].reshape(
                ranks, 2 * owned, tokens
            )
        if (i + 2) % CHUNK == 0:
            chunk = i // CHUNK
            send_all(2 + chunk, piece(tri_send, chunk), piece(tri_buf, chunk))

    last = 2 + rows // CHUNK - 1
    pair_normed = pair_normed_ref[...].reshape(rows * tokens, pair_channels)
    logits = matmul(head_w_ref[...], pair_normed, 1, 1)
    logits = jnp.concatenate(
        [logits[:, i * tokens : (i + 1) * tokens] for i in range(rows)], axis=0
    )
    powers = jnp.exp(logits - jnp.max(logits, axis=1, keepdims=True))
    weight_buf[me] = (powers / jnp.sum(powers, axis=1, keepdims=True)).astype(BF16)
    gather_start(1 + last, weight_buf)
    tri_f32[me] = tri_send[me].astype(F32).reshape(tri_f32.shape[1:])
    tri_gate = jax.nn.sigmoid(matmul(pair_normed, tri_gate_w_ref[...], 1, 0))

    for chunk in range(rows // CHUNK):
        part = 2 * owned * CHUNK

        def widen(origin, chunk=chunk, part=part):
            tri_f32[origin, chunk * part : (chunk + 1) * part] = (
                tri_buf[origin, chunk * CHUNK : (chunk + 1) * CHUNK]
                .astype(F32)
                .reshape(part, tokens)
            )

        receive_all(2 + chunk, piece(tri_send, chunk), piece(tri_buf, chunk), widen)
    tri_flat = tri_f32.reshape(ranks * rows * 2 * owned, tokens)
    sums = []
    for c in range(owned):
        sides = [
            tri_flat[pl.ds(n * owned + c, tokens, stride=2 * owned), :].astype(BF16)
            for n in range(2)
        ]
        sums.append(matmul(sides[0], sides[1], 1, 1).reshape(ranks, rows, tokens))
        if c % 2 == 1:
            back_send[:, (c - 1) * rows : (c + 1) * rows] = jnp.concatenate(
                sums[-2:], axis=1
            ).astype(BF16)
    back = (lambda rank: back_send.at[rank], lambda rank: back_buf.at[rank])
    send_all(2 + last, *back)
    gather_forward(1 + last, weight_buf)
    back_f32[me] = back_send[me].astype(F32)

    gather_finish(1 + last, weight_buf, weight_f32)
    weight_flat = weight_f32.reshape(ranks * rows * heads, tokens)
    averaged = [[] for _ in range(seqs)]
    for h in range(heads):
        weights = weight_flat[pl.ds(h, tokens, stride=heads), :].astype(BF16)
        part = values[h * head_dim : (h + 1) * head_dim]
        part = jnp.concatenate(
            [part[:, s * tokens : (s + 1) * tokens] for s in range(seqs)], axis=0
        )
        result = matmul(part, weights, 1, 1)
        for s in range(seqs):
            averaged[s].append(result[s * head_dim : (s + 1) * head_dim])
    gated = (
        gates
        * jnp.concatenate([jnp.concatenate(one, axis=0) for one in averaged], axis=1)
    ).astype(BF16)
    update = matmul(average_w_ref[...], gated, 1, 0)
    for s in range(seqs):
        msa_out_ref[s] = (
            starts[s].astype(F32) + update[:, s * tokens : (s + 1) * tokens]
        ).astype(BF16)


    def widen_back(origin):
        back_f32[origin] = back_buf[origin].astype(F32)

    receive_all(2 + last, *back, widen_back)
    back_flat = back_f32.reshape(tri_channels * rows, tokens)
    for i in range(rows):
        one = back_flat[pl.ds(i, tri_channels, stride=rows), :]
        tri_normed = layer_normalize(one, 0).astype(BF16)
        update = matmul(tri_normed, tri_out_w_ref[...], 0, 0)
        pair_out_ref[i] = (
            pair_mid_ref[i].astype(F32) + tri_gate[i * tokens : (i + 1) * tokens] * update
        ).astype(BF16)
    gather_drain(0, right_buf)
    drain(1, *left_refs)
    for chunk in range(rows // CHUNK):
        drain(2 + chunk, piece(tri_send, chunk), piece(tri_buf, chunk))
    gather_drain(1 + last, weight_buf)
    drain(2 + last, *back)


def local(ranks, *arguments):
    (
        alignment_features,
        pair_features,
        token_residue_kind,
        alignment_mask,
        residue_embedding_table,
        outer_left_weight,
        outer_right_weight,
        outer_output_weight,
        averaging_value_weight,
        averaging_gate_weight,
        averaging_head_logits,
        averaging_output_weight,
        triangle_projection_weight,
        triangle_gate_weight,
        triangle_output_weight,
    ) = arguments
    seqs, tokens, channels = alignment_features.shape
    rows, _, pair_channels = pair_features.shape
    tri_channels = triangle_output_weight.shape[0]
    width = outer_left_weight.shape[1]
    heads = averaging_head_logits.shape[1]
    owned = tri_channels // ranks
    if (2 * owned) % 16 or rows != 8 or heads != 8 or (seqs * ranks) % 16 or seqs * width > 128 or ranks % PLANE:
        return local_large(*arguments)
    sequences = seqs * ranks
    vmem = pl.BlockSpec(memory_space=pltpu.VMEM)
    operands = (
        jnp.swapaxes(alignment_features, 1, 2),
        pair_features,
        token_residue_kind.reshape(1, tokens),
        alignment_mask.reshape(1, sequences),
        residue_embedding_table,
        outer_left_weight.T,
        outer_right_weight.T,
        outer_output_weight,
        averaging_value_weight,
        averaging_gate_weight,
        averaging_head_logits.T,
        averaging_output_weight.T,
        triangle_projection_weight,
        triangle_gate_weight,
        triangle_output_weight,
    )
    msa_out, pair_out = pl.pallas_call(
        functools.partial(fused_kernel, ranks),
        out_shape=(
            jax.ShapeDtypeStruct((seqs, channels, tokens), BF16),
            jax.ShapeDtypeStruct((rows, tokens, pair_channels), BF16),
        ),
        in_specs=[pl.BlockSpec(memory_space=pl.ANY)] * len(operands),
        out_specs=(vmem, vmem),
        scratch_shapes=[
            *[pltpu.VMEM(operand.shape, operand.dtype) for operand in operands],
            pltpu.VMEM((width * width, pair_channels), F32),
            pltpu.VMEM((ranks, rows, 128), F32),
            pltpu.VMEM((ranks, rows, 128), F32),
            pltpu.VMEM((ranks, seqs * width, tokens), BF16),
            pltpu.VMEM((ranks, seqs * width, tokens), F32),
            pltpu.VMEM((width * sequences, tokens), BF16),
            pltpu.VMEM((width * sequences, rows * pair_channels), BF16),
            pltpu.VMEM((rows, tokens, pair_channels), BF16),
            pltpu.VMEM((rows, tokens, pair_channels), BF16),
            pltpu.VMEM((ranks, rows * heads, tokens), BF16),
            pltpu.VMEM((ranks, rows * heads, tokens), F32),
            pltpu.VMEM((ranks, rows, 2 * owned, tokens), BF16),
            pltpu.VMEM((ranks, rows, 2 * owned, tokens), BF16),
            pltpu.VMEM((ranks, rows * 2 * owned, tokens), F32),
            pltpu.VMEM((ranks, owned * rows, tokens), BF16),
            pltpu.VMEM((ranks, owned * rows, tokens), BF16),
            pltpu.VMEM((ranks, owned * rows, tokens), F32),
            pltpu.SemaphoreType.DMA((len(operands),)),
            pltpu.SemaphoreType.DMA((4 + rows // CHUNK, ranks)),
            pltpu.SemaphoreType.DMA((4 + rows // CHUNK, ranks)),
        ],
        compiler_params=pltpu.CompilerParams(
            collective_id=0, has_side_effects=True, vmem_limit_bytes=60 * 2**20
        ),
    )(*operands)
    return jnp.swapaxes(msa_out, 1, 2), pair_out


def solution(mesh):
    placed = (
        P(("groups", "row"), None, None),
        P(("groups", "row"), None, None),
        P("groups"),
        P("groups"),
        P(),
        P(),
        P(),
        P(),
        P(),
        P(),
        P(),
        P(),
        P(),
        P(),
        P(),
    )
    return jax.shard_map(
        functools.partial(local, mesh.shape["row"]),
        mesh=mesh,
        in_specs=placed,
        out_specs=(P(("groups", "row"), None, None), P(("groups", "row"), None, None)),
        check_vma=False,
    )
```
